256 devices in a mesh: role: 2 (over y_lo), grp: 8 (over z), tp: 16 (over x, y_hi, core).
Axes of the slice: x: 4, y: 4 (y_hi: 2, y_lo: 2; y = y_hi * 2 + y_lo), z: 8, core: 2. Of those that a mesh axis runs over, the one named last changes fastest.
Arguments:
- hidden: bfloat16 [2, 8, 64, 8192], P('role', 'grp', 'tp'), may hold values from -6 to 6
- norm_gain: float32 [8192], replicated, may hold values from 0.1 to 1.9
- w_query: bfloat16 [8192, 4096], P(None, 'tp'), may hold values from -0.0625 to 0.0625
- w_keyval: bfloat16 [8192, 1024], P(None, 'tp'), may hold values from -0.16992188 to 0.16992188
- w_out: bfloat16 [4096, 8192], P('tp'), may hold values from -0.09375 to 0.09375
- kv_cache: bfloat16 [2, 8, 4096, 1024], P('role', 'grp', None, 'tp'), may hold values from -180 to 180
- match: int32 [8], replicated, may hold values from 0 to 7, as said below
- cache_lengths: int32 [8, 31], P('grp'), may hold values from 1 to 256, 4096 in all within a row
Outputs:
- layer_out: bfloat16 [2, 8, 64, 8192], P('role', 'grp', 'tp')
The draws below stay inside these ranges and needn't reach their ends.
Inputs may be any that keep to these rules, and one draw needn't show every extreme that they name: `match`: a permutation of the groups in which prefill group 8 - 1 hands over to decode group 0. `cache_lengths`: each row sums to 4096, and its largest entry is exactly 256.
All inputs are finite; a program needn't handle non-finite values.
Results may differ from the reference program's by a relative error of at most 0.03.
Values may be sent and summed in bfloat16 or wider, within the bound.
No kernel may reach another device: no remote copies, remote signals or barrier semaphores. Data moves between devices by JAX's collectives and lax.ppermute only.
A program may use at most 64 MiB of HBM per device.

```python
import math
import jax
import jax.numpy as jnp
import numpy as np
from jax import lax

D = 8192
HQ = 32
KVH = 4
HD = 128
REQ = 32
STEPS = 2
ROWS = 64
CT = 4096
LMAX = 256
GRP = 8


def draw_kv_cache(key, part):
    key = jax.random.fold_in(key, 11)
    columns = 2 * KVH * HD
    shape = (2, GRP, CT, columns)
    scaled = 2.5 * jnp.clip(jax.random.normal(key, shape, jnp.float32), -6.0, 6.0)
    return scaled.astype(jnp.bfloat16)


def draw_match(key, part):
    key = jax.random.fold_in(key, 23)
    shuffled = jax.random.permutation(key, GRP).astype(jnp.int32)
    last_entry = shuffled[GRP - 1]
    swapped = jnp.where(shuffled == 0, last_entry, shuffled)
    return swapped.at[GRP - 1].set(0).astype(jnp.int32)


def block_levels(own_key, shape, cuts, smallest, high):
    gain = 1.0
    for position, parts in cuts:
        draws = jax.random.uniform(jax.random.fold_in(jax.random.fold_in(own_key, 6), position), (parts,), jnp.float32, smallest / len(cuts), high / len(cuts))
        gain = gain * jnp.repeat(jnp.exp(draws), shape[position] // parts).reshape((-1,) + (1,) * (len(shape) - 1 - position))
    return gain


def profile(count, total, most, skew):
    loads = [(1 << 20) // math.isqrt(standing ** skew) + 1 for standing in range(2, count + 1)]
    rest, given = total - most - (count - 1), [1] * (count - 1)
    while rest > 0:
        candidates = [i for i in range(count - 1) if given[i] < most]
        whole, remaining = sum([loads[i] for i in candidates]), rest
        for i in candidates:
            more = min(most - given[i], max(1, remaining * loads[i] // whole), rest)
            given[i] = given[i] + more
            rest = rest - more
    return np.array([most] + given)


def uneven(key, amount, total, reach, lean):
    if amount == 2:
        one = jax.random.randint(key, (), max(1, total - reach), min(reach, total - 1) + 1)
        return jnp.stack([one, total - one])
    lengths = jnp.asarray(profile(amount, total, reach, lean), jnp.int32)
    pairs = (amount - 1) // 2
    giver, receiver = lengths[1:1 + 2 * pairs:2], lengths[2:2 + 2 * pairs:2]
    slack = jnp.minimum(giver - 1, reach - receiver)
    shifted = jax.random.randint(jax.random.fold_in(key, 1), (pairs,), 0, 1 << 20) % (slack + 1)
    lengths = lengths.at[1:1 + 2 * pairs:2].set(giver - shifted).at[2:2 + 2 * pairs:2].set(receiver + shifted)
    return lengths[jax.random.permutation(jax.random.fold_in(key, 2), amount)]


def scatter_about(rng, extent, scale, limit, cuts=(), kind=jnp.bfloat16):
    level = block_levels(rng, extent, cuts, -0.22, 0.18) if cuts else 1.0
    entries = jax.random.normal(rng, extent, jnp.float32) * scale * level
    return jnp.minimum(jnp.maximum(entries, -limit), limit).astype(kind)


def setup_inputs(seed: int = 0) -> dict:
    arg_keys = jax.random.split(jax.random.key(seed), 9)
    hidden = scatter_about(arg_keys[0], (2, GRP, ROWS, D), 1.0, 6.0, ((0, 2), (1, 8), (2, 16)))
    norm_gain = jnp.clip(1.0 + 0.18 * jax.random.normal(arg_keys[1], (D,), jnp.float32), 0.1, 1.9)
    w_query = scatter_about(arg_keys[2], (D, HQ * HD), D ** -0.5, 0.0625, ((1, 16),))
    w_keyval = scatter_about(arg_keys[3], (D, 2 * KVH * HD), 0.0276, 0.16992188, ((1, 16),))
    w_out = scatter_about(arg_keys[4], (HQ * HD, D), (HQ * HD) ** -0.5, 0.09375, ((0, 16),))
    kv_cache = draw_kv_cache(jax.random.fold_in(arg_keys[8], 71), 0)
    match = draw_match(jax.random.fold_in(arg_keys[8], 71), 0)
    cache_lengths = jax.vmap(lambda own: uneven(own, REQ - 1, CT, LMAX, 2))(jax.random.split(arg_keys[7], GRP)).reshape((GRP, REQ - 1)).astype(jnp.int32)
    return {"hidden": hidden, "norm_gain": norm_gain, "w_query": w_query, "w_keyval": w_keyval, "w_out": w_out, "kv_cache": kv_cache, "match": match, "cache_lengths": cache_lengths}


def rotate(tensor, positions):
    half_dim = HD // 2
    inverse = 500000.0 ** (-(2.0 / HD) * jnp.arange(half_dim, dtype=jnp.float32))
    angles = positions.astype(jnp.float32)[:, None] * inverse[None, :]
    cosine = jnp.cos(angles)[:, None, :]
    sine = jnp.sin(angles)[:, None, :]
    paired = tensor.reshape(tensor.shape[0], tensor.shape[1], half_dim, 2)
    first = paired[..., 0]
    second = paired[..., 1]
    turned = jnp.stack([first * cosine - second * sine, first * sine + second * cosine], -1)
    return turned.reshape(tensor.shape)

def project(hidden_rows, norm_gain, w_query, w_keyval, positions):
    floated = hidden_rows.astype(jnp.float32)
    spread = lax.optimization_barrier(jnp.mean(floated * floated, axis=-1, keepdims=True))
    normed = (floated * lax.rsqrt(spread + 1e-05) * norm_gain).astype(jnp.bfloat16)
    row_count = hidden_rows.shape[0]
    query = jnp.dot(normed, w_query, preferred_element_type=jnp.float32).reshape(row_count, HQ, HD)
    query = rotate(query, positions).astype(jnp.bfloat16)
    keyval = jnp.dot(normed, w_keyval, preferred_element_type=jnp.float32).reshape(row_count, KVH, 2, HD)
    fresh_keys = rotate(keyval[:, :, 0], positions).astype(jnp.bfloat16)
    fresh_values = keyval[:, :, 1].astype(jnp.bfloat16)
    return (query, fresh_keys, fresh_values)

def split_cache(block):
    shaped = block.reshape(block.shape[0], KVH, 2, HD)
    return (shaped[:, :, 0], shaped[:, :, 1])

def attend(query, key_set, value_set, allowed):
    row_count = query.shape[0]
    grouped = query.reshape(row_count, KVH, HQ // KVH, HD).astype(jnp.float32)
    scores = jnp.einsum('rkgd,tkd->kgrt', grouped, key_set.astype(jnp.float32)) / math.sqrt(HD)
    scores = jnp.where(allowed[None, None], scores, -jnp.inf)
    peak = lax.optimization_barrier(jnp.max(scores, -1, keepdims=True))
    weights = jnp.exp(scores - peak)
    probs = (weights / lax.optimization_barrier(jnp.sum(weights, -1, keepdims=True))).astype(jnp.bfloat16)
    mixed = jnp.einsum('kgrt,tkd->rkgd', probs.astype(jnp.float32), value_set.astype(jnp.float32))
    return mixed.reshape(row_count, HQ * HD).astype(jnp.bfloat16)

def finish(hidden_rows, attended, w_out):
    summed = jnp.dot(attended, w_out, preferred_element_type=jnp.float32)
    return (hidden_rows.astype(jnp.float32) + summed).astype(jnp.bfloat16)

def reference(hidden, norm_gain, w_query, w_keyval, w_out, kv_cache, match, cache_lengths):
    row_ids = jnp.arange(ROWS, dtype=jnp.int32)
    request = row_ids // STEPS
    step_ids = row_ids % STEPS
    prompt_keys = []
    prompt_values = []
    results_pre = []
    for group in range(GRP):
        positions = CT + row_ids
        query, fresh_keys, fresh_values = project(hidden[0, group], norm_gain, w_query, w_keyval, positions)
        cached_keys, cached_values = split_cache(kv_cache[0, group])
        key_set = jnp.concatenate([cached_keys, fresh_keys], 0)
        value_set = jnp.concatenate([cached_values, fresh_values], 0)
        allowed = jnp.arange(CT + ROWS, dtype=jnp.int32)[None, :] <= CT + row_ids[:, None]
        results_pre.append(finish(hidden[0, group], attend(query, key_set, value_set, allowed), w_out))
        prompt_keys.append(key_set)
        prompt_values.append(value_set)
    stacked_keys = jnp.stack(prompt_keys)
    stacked_values = jnp.stack(prompt_values)
    results_dec = []
    for group in range(GRP):
        source = jnp.sum(jnp.where(match == group, jnp.arange(GRP, dtype=jnp.int32), 0)).astype(jnp.int32)
        arrived_keys = lax.dynamic_index_in_dim(stacked_keys, source, 0, keepdims=False)
        arrived_values = lax.dynamic_index_in_dim(stacked_values, source, 0, keepdims=False)
        lengths_row = cache_lengths[group].astype(jnp.int32)
        bases = jnp.concatenate([jnp.full((1,), CT + ROWS, jnp.int32), lengths_row])
        positions = bases[request] + step_ids
        query, fresh_keys, fresh_values = project(hidden[1, group], norm_gain, w_query, w_keyval, positions)
        cached_keys, cached_values = split_cache(kv_cache[1, group])
        key_set = jnp.concatenate([arrived_keys, cached_keys, fresh_keys], 0)
        value_set = jnp.concatenate([arrived_values, cached_values, fresh_values], 0)
        offsets = (jnp.cumsum(lengths_row) - lengths_row).astype(jnp.int32)
        zero_one = jnp.zeros((1,), jnp.int32)
        starts = jnp.concatenate([zero_one, offsets])[request]
        spans = jnp.concatenate([zero_one, lengths_row])[request]
        arrived_ok = jnp.broadcast_to((request == 0)[:, None], (ROWS, CT + ROWS))
        cache_index = jnp.arange(CT, dtype=jnp.int32)[None, :]
        cache_ok = (cache_index >= starts[:, None]) & (cache_index < (starts + spans)[:, None])
        new_index = row_ids[None, :]
        new_ok = (new_index // STEPS == request[:, None]) & (new_index % STEPS <= step_ids[:, None])
        allowed = jnp.concatenate([arrived_ok, cache_ok, new_ok], 1)
        results_dec.append(finish(hidden[1, group], attend(query, key_set, value_set, allowed), w_out))
    return jnp.stack([jnp.stack(results_pre), jnp.stack(results_dec)])
```

```python
import math

import jax
import jax.numpy as jnp
from jax import lax
from jax.experimental import pallas as pl
from jax.experimental.pallas import tpu as pltpu
from jax.sharding import PartitionSpec as P

HD = 128
STEPS = 2
XN = 4
NEG = -math.inf
F32 = jnp.float32
BF16 = jnp.bfloat16
VMEM = pl.BlockSpec(memory_space=pltpu.VMEM)

CORE = [(i, i ^ 1) for i in range(16)]
YHI = [(i, i ^ 2) for i in range(16)]
BOTH = [(i, i ^ 3) for i in range(16)]


def xshift(k):
    return [(i, (i + 4 * k) % 16) for i in range(16)]


def after(value, *others):
    return lax.optimization_barrier((value,) + others)[0]


def norm_kernel(hidden_ref, gain_ref, out_ref):
    floated = hidden_ref[...].astype(F32)
    spread = jnp.mean(floated * floated, axis=-1, keepdims=True)
    out_ref[...] = (floated * lax.rsqrt(spread + 1e-05) * gain_ref[...]).astype(BF16)


def norm(rows, gain):
    return pl.pallas_call(
        norm_kernel,
        out_shape=jax.ShapeDtypeStruct(rows.shape, BF16),
        in_specs=[VMEM, VMEM],
        out_specs=VMEM,
    )(rows, gain[None, :])


def turn(value, cosine, sine, axis):
    size = value.shape[axis]
    index = lax.broadcasted_iota(jnp.int32, value.shape, axis)
    ahead = pltpu.roll(value, size - 1, axis)
    behind = pltpu.roll(value, 1, axis)
    return value * cosine + jnp.where(index % 2 == 0, ahead, behind) * sine


def project_kernel(
    own_ref, mate_ref, wq_ref, wkv_ref, cq_ref, sq_ref, ck_ref, sk_ref, perm_ref,
    q_ref, fresh_ref, accq, acck,
):
    step = pl.program_id(0)

    @pl.when(step == 0)
    def _():
        accq[...] = jnp.zeros_like(accq)
        acck[...] = jnp.zeros_like(acck)

    rows = jnp.concatenate([own_ref[...], mate_ref[...]], 0)
    accq[...] += jnp.dot(rows, wq_ref[...], preferred_element_type=F32)
    acck[...] += lax.dot_general(
        wkv_ref[...], rows, (((1,), (1,)), ((), ())), preferred_element_type=F32
    )

    @pl.when(step == pl.num_programs(0) - 1)
    def _():
        perm = perm_ref[...]
        query = turn(accq[...], cq_ref[...], sq_ref[...], 1).astype(BF16)
        q_ref[...] = jnp.dot(perm, query, preferred_element_type=F32).astype(BF16)
        fresh = turn(acck[...], ck_ref[...], sk_ref[...], 0).astype(BF16)
        fresh_ref[...] = lax.dot_general(
            fresh, perm, (((1,), (1,)), ((), ())), preferred_element_type=F32
        ).astype(BF16)


def project(own, mate, w_query, w_kv_t, cq, sq, ck, sk, perm):
    half, depth = own.shape
    rows = 2 * half
    qcols = w_query.shape[1]
    kcols = w_kv_t.shape[0]
    chunk = 2048
    full = lambda shape: pl.BlockSpec(shape, lambda k: (0, 0))
    return pl.pallas_call(
        project_kernel,
        grid=(depth // chunk,),
        out_shape=(
            jax.ShapeDtypeStruct((rows, qcols), BF16),
            jax.ShapeDtypeStruct((kcols, rows), BF16),
        ),
        in_specs=[
            pl.BlockSpec((half, chunk), lambda k: (0, k)),
            pl.BlockSpec((half, chunk), lambda k: (0, k)),
            pl.BlockSpec((chunk, qcols), lambda k: (k, 0)),
            pl.BlockSpec((kcols, chunk), lambda k: (0, k)),
            full((rows, qcols)),
            full((rows, qcols)),
            full((kcols, rows)),
            full((kcols, rows)),
            full((rows, rows)),
        ],
        out_specs=(full((rows, qcols)), full((kcols, rows))),
        scratch_shapes=[pltpu.VMEM((rows, qcols), F32), pltpu.VMEM((kcols, rows), F32)],
        compiler_params=pltpu.CompilerParams(vmem_limit_bytes=16 * 1024 * 1024),
    )(own, mate, w_query, w_kv_t, cq, sq, ck, sk, perm)


def softmax_parts(queries, bounds_ref, me, kv_ref, fresh_ref, scores):
    tokens = kv_ref.shape[2]
    chunk = 512
    scale = 1.0 / math.sqrt(HD)
    bounds = bounds_ref[...]
    low, high, fresh_low, fresh_high = (bounds[:, i : i + 1] for i in range(4))
    part = [jnp.bitwise_xor(me, i) for i in range(4)]

    def pair(ref, first, span):
        return jnp.concatenate([ref[part[first], :, span], ref[part[first + 1], :, span]], 0)

    whole = slice(None)
    fresh_scores = jnp.dot(queries, pair(fresh_ref, 0, whole), preferred_element_type=F32) * scale
    index = lax.broadcasted_iota(jnp.int32, fresh_scores.shape, 1)
    fresh_scores = jnp.where((index >= fresh_low) & (index <= fresh_high), fresh_scores, NEG)
    peak = jnp.max(fresh_scores, -1, keepdims=True)
    for start in range(0, tokens, chunk):
        span = slice(start, start + chunk)
        part_scores = jnp.dot(queries, pair(kv_ref, 0, span), preferred_element_type=F32) * scale
        index = lax.broadcasted_iota(jnp.int32, part_scores.shape, 1) + start
        part_scores = jnp.where((index >= low) & (index < high), part_scores, NEG)
        scores[:, span] = part_scores
        peak = jnp.maximum(peak, jnp.max(part_scores, -1, keepdims=True))
    contract = (((1,), (1,)), ((), ()))
    weights = jnp.exp(fresh_scores - peak)
    total = jnp.sum(weights, -1, keepdims=True)
    mixed = lax.dot_general(
        weights.astype(BF16), pair(fresh_ref, 2, whole), contract, preferred_element_type=F32
    )
    for start in range(0, tokens, chunk):
        span = slice(start, start + chunk)
        weights = jnp.exp(scores[:, span] - peak)
        total += jnp.sum(weights, -1, keepdims=True)
        mixed += lax.dot_general(
            weights.astype(BF16), pair(kv_ref, 2, span), contract, preferred_element_type=F32
        )
    return mixed, peak, total


def two_heads(query):
    return jnp.concatenate([query[:, :HD], query[:, HD:]], 0)


def pack_parts(mixed, peak, total):
    spread = lambda column: jnp.broadcast_to(column, mixed.shape)
    return jnp.concatenate([mixed, spread(peak), spread(total)], 1)


def main_kernel(me_ref, q_ref, bounds_ref, kv_ref, fresh_ref, perm_ref, out_ref, first_ref, scores):
    query = q_ref[...]
    rows = query.shape[0]
    mixed, peak, total = softmax_parts(
        two_heads(query), bounds_ref, me_ref[0], kv_ref, fresh_ref, scores
    )
    ready = mixed / total
    attended = jnp.concatenate([ready[:rows], ready[rows:]], 1).astype(BF16)
    out_ref[...] = lax.dot_general(
        perm_ref[...], attended, (((0,), (0,)), ((), ())), preferred_element_type=F32
    ).astype(BF16)
    packed = pack_parts(mixed, peak, total)
    first_ref[...] = jnp.concatenate([packed[:8], packed[rows : rows + 8]], 0)


def first_kernel(me_ref, q_ref, bounds_ref, kv_ref, fresh_ref, out_ref, scores):
    mixed, peak, total = softmax_parts(
        two_heads(q_ref[...]), bounds_ref, me_ref[0], kv_ref, fresh_ref, scores
    )
    out_ref[...] = pack_parts(mixed, peak, total)


SMEM = pl.BlockSpec(memory_space=pltpu.SMEM)
LIMIT = pltpu.CompilerParams(vmem_limit_bytes=24 * 1024 * 1024)


def attend_main(me, query, bounds, kv, fresh, perm):
    rows = query.shape[0]
    return pl.pallas_call(
        main_kernel,
        out_shape=(
            jax.ShapeDtypeStruct(query.shape, BF16),
            jax.ShapeDtypeStruct((16, 3 * HD), F32),
        ),
        in_specs=[SMEM, VMEM, VMEM, VMEM, VMEM, VMEM],
        out_specs=(VMEM, VMEM),
        scratch_shapes=[pltpu.VMEM((2 * rows, kv.shape[2]), F32)],
        compiler_params=LIMIT,
    )(me, query, bounds, kv, fresh, perm)


def attend_first(me, query, bounds, kv, fresh):
    return pl.pallas_call(
        first_kernel,
        out_shape=jax.ShapeDtypeStruct((2 * query.shape[0], 3 * HD), F32),
        in_specs=[SMEM, VMEM, VMEM, VMEM, VMEM],
        out_specs=VMEM,
        scratch_shapes=[pltpu.VMEM((2 * query.shape[0], kv.shape[2]), F32)],
        compiler_params=LIMIT,
    )(me, query, bounds, kv, fresh)


def merge_kernel(own_ref, far_ref, w_ref, out_ref):
    own = own_ref[...]
    far = far_ref[...]
    split = lambda packed: (packed[:, :HD], packed[:, HD : 2 * HD], packed[:, 2 * HD :])
    mixed_a, peak_a, total_a = split(own)
    mixed_b, peak_b, total_b = split(far)
    peak = jnp.maximum(peak_a, peak_b)
    scale_a = jnp.exp(peak_a - peak)
    scale_b = jnp.exp(peak_b - peak)
    ready = (mixed_a * scale_a + mixed_b * scale_b) / (total_a * scale_a + total_b * scale_b)
    attended = jnp.concatenate([ready[:8], ready[8:]], 1).astype(BF16)
    out_ref[...] = jnp.dot(attended, w_ref[...], preferred_element_type=F32).astype(BF16)


def merge(own, far, w_out):
    return pl.pallas_call(
        merge_kernel,
        out_shape=jax.ShapeDtypeStruct((8, w_out.shape[1]), BF16),
        in_specs=[VMEM, VMEM, VMEM],
        out_specs=VMEM,
        compiler_params=LIMIT,
    )(own, far, w_out)


def pick_row(table, selector):
    return jnp.sum(jnp.where(selector, table[None, :], 0), 1)


def local(hidden, norm_gain, w_query, w_keyval, w_out, kv_cache, match, cache_lengths):
    side = lax.axis_index("role")
    group = lax.axis_index("grp")
    tp = lax.axis_index("tp")
    own_rows = hidden[0, 0]
    block = own_rows.shape[0]
    row_count = block * lax.axis_size("tp")
    kv_t = kv_cache[0, 0].T
    cache_len = kv_t.shape[1]
    qcols = w_query.shape[1]
    kcols = w_keyval.shape[1]

    normed = norm(own_rows, norm_gain)
    beside = lax.ppermute(normed, "tp", YHI)
    kv_own = after(kv_t, beside)
    kv_core = lax.ppermute(kv_own, "tp", CORE)
    pair = jnp.concatenate([normed, beside], 0)
    pair = after(pair)
    others = [lax.ppermute(pair, "tp", xshift(-k)) for k in range(1, XN)]
    kv_y = lax.ppermute(kv_own, "tp", YHI)
    own_half = after(jnp.concatenate([pair] + others, 0))
    mate_half = lax.ppermute(own_half, "tp", CORE)
    kv_both = lax.ppermute(kv_y, "tp", CORE)
    kv = jnp.stack([kv_own, kv_core, kv_y, kv_both])

    slot = jnp.arange(row_count, dtype=jnp.int32)
    piece = slot // block
    far_core, far_x, far_y = piece // 8, piece // 2 % XN, piece % 2
    owner = (
        (tp // 4 + far_x) % XN * 4
        + jnp.bitwise_xor(tp // 2 % 2, far_y) * 2
        + jnp.bitwise_xor(tp % 2, far_core)
    )
    row_at = owner * block + slot % block
    row_ids = jnp.arange(row_count, dtype=jnp.int32)
    placed = row_at[None, :] == row_ids[:, None]
    perm = placed.astype(BF16)

    request = row_ids // STEPS
    step_ids = row_ids % STEPS
    lengths = cache_lengths[0]
    zero_one = jnp.zeros((1,), jnp.int32)
    bases = jnp.concatenate([jnp.full((1,), cache_len + row_count, jnp.int32), lengths])
    offsets = jnp.cumsum(lengths) - lengths
    selector = request[:, None] == jnp.arange(row_count // STEPS, dtype=jnp.int32)[None, :]
    start = pick_row(jnp.concatenate([zero_one, offsets]), selector)
    span = pick_row(jnp.concatenate([zero_one, lengths]), selector)
    positions = jnp.where(side == 0, cache_len + row_ids, pick_row(bases, selector) + step_ids)
    low = jnp.where(side == 0, 0, start)
    high = jnp.where(side == 0, cache_len, start + span)
    fresh_low = jnp.where(side == 0, 0, request * STEPS)
    bounds = jnp.stack([low, high, fresh_low, row_ids], 1)
    bounds = jnp.concatenate([bounds, bounds], 0)
    first_bounds = jnp.broadcast_to(
        jnp.array([0, cache_len, 0, row_count - 1], jnp.int32)[None, :], (16, 4)
    )

    position_at = jnp.sum(jnp.where(placed, positions[:, None], 0), 0).astype(F32)
    column = jnp.arange(qcols, dtype=jnp.int32)
    inverse = 500000.0 ** (-(2.0 / HD) * (column % HD // 2).astype(F32))
    angles = position_at[:, None] * inverse[None, :]
    cq = jnp.cos(angles)
    sq = jnp.sin(angles) * jnp.where(column % 2 == 0, -1.0, 1.0)[None, :]
    column = tp * kcols + jnp.arange(kcols, dtype=jnp.int32)
    inverse = 500000.0 ** (-(2.0 / HD) * (column % HD // 2).astype(F32))
    angles = inverse[:, None] * position_at[None, :]
    is_key = (column // HD % 2 == 0)[:, None]
    ck = jnp.where(is_key, jnp.cos(angles), 1.0)
    sk = jnp.where(is_key, jnp.sin(angles) * jnp.where(column % 2 == 0, -1.0, 1.0)[:, None], 0.0)

    query, fresh_own = project(
        own_half, mate_half, w_query, w_keyval.T, cq, sq, ck, sk, perm
    )

    sides = lax.axis_size("role") * lax.axis_size("grp")
    asked = lax.all_to_all(
        jnp.broadcast_to(query[None, :8], (sides, 8, qcols)), ("role", "grp"), 0, 0
    )
    fresh = jnp.stack(
        [fresh_own] + [lax.ppermute(fresh_own, "tp", route) for route in (CORE, YHI, BOTH)]
    )
    me = jnp.reshape(tp % 4, (1,)).astype(jnp.int32)
    attended, first_own = attend_main(me, query, bounds, kv, fresh, perm)
    target = pick_row(match, (jnp.arange(match.shape[0]) == group)[None, :])[0]
    source = jnp.sum(jnp.where(match == group, jnp.arange(match.shape[0], dtype=jnp.int32), 0))
    mine = lax.dynamic_index_in_dim(asked, match.shape[0] + target, 0, keepdims=False)
    told = attend_first(me, mine, first_bounds, kv, fresh)
    answers = lax.all_to_all(
        jnp.broadcast_to(told[None], (sides,) + told.shape), ("role", "grp"), 0, 0
    )

    shares = jnp.dot(attended, w_out, preferred_element_type=F32).astype(BF16)
    half = row_count // 2
    across = lax.ppermute(shares[half:], "tp", CORE)
    total = (shares[:half].astype(F32) + across.astype(F32)).astype(BF16)
    width = half // XN
    parts = [
        lax.ppermute(total[k * width : (k + 1) * width], "tp", xshift(k)) for k in range(1, XN)
    ]
    total = total[:width].astype(F32)
    for part in parts:
        total = total + part.astype(F32)
    total = total.astype(BF16)
    across = lax.ppermute(total[block:], "tp", YHI)
    summed = total[:block].astype(F32) + across.astype(F32)

    far = lax.dynamic_index_in_dim(answers, source, 0, keepdims=False)
    lead = merge(first_own, far, w_out)[:STEPS]
    lead = (lead.astype(F32) + lax.ppermute(lead, "tp", CORE).astype(F32)).astype(BF16)
    lead = (lead.astype(F32) + lax.ppermute(lead, "tp", YHI).astype(F32)).astype(BF16)
    parts = [lax.ppermute(lead, "tp", xshift(k)) for k in range(1, XN)]
    lead = lead.astype(F32)
    for part in parts:
        lead = lead + part.astype(F32)
    lead = jnp.concatenate([lead, summed[STEPS:]], 0)
    summed = jnp.where((side == 1) & (tp == 0), lead, summed)
    return (own_rows.astype(F32) + summed).astype(BF16)[None, None]


def solution(mesh):
    return jax.shard_map(
        local,
        mesh=mesh,
        in_specs=(
            P("role", "grp", "tp", None),
            P(),
            P(None, "tp"),
            P(None, "tp"),
            P("tp", None),
            P("role", "grp", None, "tp"),
            P(),
            P("grp", None),
        ),
        out_specs=P("role", "grp", "tp", None),
        check_vma=False,
    )
```

```python
import functools
import math

import jax
import jax.numpy as jnp
from jax import lax
from jax.experimental import pallas as pl
from jax.experimental.pallas import tpu as pltpu
from jax.sharding import PartitionSpec as P

HD = 128
STEPS = 2
XN = 4
NEG = -math.inf
F32 = jnp.float32
BF16 = jnp.bfloat16
VMEM = pl.BlockSpec(memory_space=pltpu.VMEM)
COST = pl.CostEstimate(flops=1, bytes_accessed=1, transcendentals=0)

CORE = [(i, i ^ 1) for i in range(16)]
YHI = [(i, i ^ 2) for i in range(16)]
BOTH = [(i, i ^ 3) for i in range(16)]


def xshift(k):
    return [(i, (i + 4 * k) % 16) for i in range(16)]


def after(value, *others):
    return lax.optimization_barrier((value,) + others)[0]


def norm_kernel(own_ref, beside_ref, gain_ref, out_ref):
    floated = jnp.concatenate([own_ref[...].astype(F32), beside_ref[...].astype(F32)], 0)
    spread = jnp.mean(floated * floated, axis=-1, keepdims=True)
    out_ref[...] = (floated * lax.rsqrt(spread + 1e-05) * gain_ref[...]).astype(BF16)


def norm(own, beside, gain):
    return pl.pallas_call(
        norm_kernel,
        cost_estimate=COST,
        out_shape=jax.ShapeDtypeStruct((2 * own.shape[0], own.shape[1]), BF16),
        in_specs=[VMEM, VMEM, VMEM],
        out_specs=VMEM,
    )(own, beside, gain[None, :])


def fetch_kernel(source_ref, out_ref, sem):
    copy = pltpu.make_async_copy(source_ref, out_ref, sem)
    copy.start()
    copy.wait()


def fetch(weights):
    return pl.pallas_call(
        fetch_kernel,
        cost_estimate=COST,
        out_shape=jax.ShapeDtypeStruct(weights.shape, weights.dtype),
        in_specs=[pl.BlockSpec(memory_space=pltpu.HBM)],
        out_specs=VMEM,
        scratch_shapes=[pltpu.SemaphoreType.DMA],
        compiler_params=pltpu.CompilerParams(vmem_limit_bytes=8 * 1024 * 1024),
    )(weights)


def turn(value, cosine, sine, axis):
    size = value.shape[axis]
    index = lax.broadcasted_iota(jnp.int32, value.shape, axis)
    ahead = pltpu.roll(value, size - 1, axis)
    behind = pltpu.roll(value, 1, axis)
    return value * cosine + jnp.where(index % 2 == 0, ahead, behind) * sine


def project_kernel(
    own_ref, mate_ref, wq_ref, wkv_ref, cq_ref, sq_ref, ck_ref, sk_ref, perm_ref,
    q_ref, pack_ref,
):
    rows = jnp.concatenate([own_ref[...], mate_ref[...]], 0)
    query = jnp.dot(rows, wq_ref[...], preferred_element_type=F32)
    fresh = lax.dot_general(
        wkv_ref[...], rows, (((1,), (1,)), ((), ())), preferred_element_type=F32
    )
    perm = perm_ref[...]
    query = turn(query, cq_ref[...], sq_ref[...], 1).astype(BF16)
    query = jnp.dot(perm, query, preferred_element_type=F32)
    q_ref[...] = query.astype(BF16)
    fresh = turn(fresh, ck_ref[...], sk_ref[...], 0).astype(BF16)
    fresh = lax.dot_general(fresh, perm, (((1,), (1,)), ((), ())), preferred_element_type=F32)
    size = fresh.shape[0]
    pack_ref[:size, :] = jnp.concatenate([fresh, jnp.zeros_like(fresh)], 1).astype(BF16)
    lead = lead_rows(query[:, :HD], query[:, HD:])
    pack_ref[size:, :] = jnp.concatenate([lead, jnp.zeros_like(lead)], 0).astype(BF16)


def lead_rows(first, second):
    both = jnp.concatenate([first[:STEPS], second[:STEPS]], 0)
    return jnp.concatenate([both, jnp.zeros_like(both)], 0)


def project(own, mate, w_query, w_kv_t, cq, sq, ck, sk, perm):
    rows = 2 * own.shape[0]
    return pl.pallas_call(
        project_kernel,
        cost_estimate=COST,
        out_shape=(
            jax.ShapeDtypeStruct((rows, w_query.shape[1]), BF16),
            jax.ShapeDtypeStruct((w_kv_t.shape[0] + 16, HD), BF16),
        ),
        in_specs=[VMEM] * 9,
        out_specs=(VMEM,) * 2,
        compiler_params=pltpu.CompilerParams(vmem_limit_bytes=16 * 1024 * 1024),
    )(own, mate, w_query, w_kv_t, cq, sq, ck, sk, perm)


def softmax_parts(queries, bounds, kv_refs, fresh, scores):
    tokens = kv_refs[0].shape[1]
    chunk = 512
    scale = 1.0 / math.sqrt(HD)
    low, high, fresh_low, fresh_high = bounds

    def pair(first, span):
        return jnp.concatenate([kv_refs[first][:, span], kv_refs[first + 1][:, span]], 0)

    fresh_keys = jnp.concatenate(fresh[:2], 0)
    fresh_values = jnp.concatenate(fresh[2:], 0)
    fresh_scores = jnp.dot(queries, fresh_keys, preferred_element_type=F32) * scale
    index = lax.broadcasted_iota(jnp.int32, fresh_scores.shape, 1)
    fresh_scores = jnp.where((index >= fresh_low) & (index <= fresh_high), fresh_scores, NEG)
    peak = jnp.max(fresh_scores, -1, keepdims=True)
    for start in range(0, tokens, chunk):
        span = slice(start, start + chunk)
        part_scores = jnp.dot(queries, pair(0, span), preferred_element_type=F32) * scale
        index = lax.broadcasted_iota(jnp.int32, part_scores.shape, 1) + start
        part_scores = jnp.where((index >= low) & (index < high), part_scores, NEG)
        scores[:, span] = part_scores
        peak = jnp.maximum(peak, jnp.max(part_scores, -1, keepdims=True))
    contract = (((1,), (1,)), ((), ()))
    weights = jnp.exp(fresh_scores - peak)
    total = jnp.sum(weights, -1, keepdims=True)
    mixed = lax.dot_general(
        weights.astype(BF16), fresh_values, contract, preferred_element_type=F32
    )
    for start in range(0, tokens, chunk):
        span = slice(start, start + chunk)
        weights = jnp.exp(scores[:, span] - peak)
        total += jnp.sum(weights, -1, keepdims=True)
        mixed += lax.dot_general(
            weights.astype(BF16), pair(2, span), contract, preferred_element_type=F32
        )
    return mixed, peak, total


def pack_parts(mixed, peak, total):
    lane = lax.broadcasted_iota(jnp.int32, mixed.shape, 1)
    return jnp.concatenate([mixed, jnp.where(lane < HD // 2, peak, total)], 1)


def in_order(place, held):
    return [held[place ^ part] for part in range(4)]


def attend_kernel(me_ref, q_ref, bounds_ref, *refs):
    kv_refs, pack_refs, asked = refs[:4], refs[4:6], refs[6:10]
    out_ref, lead_ref = refs[10:12]
    answers = refs[12:16]
    scores = refs[16]
    size = kv_refs[0].shape[0]
    other = pack_refs[0].shape[0] // 2

    def body(place):
        query = q_ref[...]
        rows = query.shape[0]
        held = [ref[first : first + size, :rows] for ref in pack_refs for first in (0, other)]
        far = []
        for ref in asked:
            both = ref[...].astype(F32)
            far += [both[:4], both[16:20]]
        far = jnp.concatenate(far, 0).astype(BF16)
        bounds = bounds_ref[...]
        mixed, peak, total = softmax_parts(
            jnp.concatenate([query[:, :HD], query[:, HD:], far], 0),
            [bounds[:, i : i + 1] for i in range(4)],
            in_order(place, kv_refs),
            in_order(place, held),
            scores,
        )
        ready = mixed / total
        out_ref[...] = jnp.concatenate([ready[:rows], ready[rows : 2 * rows]], 1).astype(BF16)
        packed = pack_parts(mixed, peak, total)
        lead_ref[...] = lead_rows(packed[:8], packed[rows : rows + 8])
        for i, ref in enumerate(answers):
            ref[...] = packed[2 * rows + 8 * i : 2 * rows + 8 * i + 8]

    for place in range(4):
        pl.when(me_ref[0] == place)(functools.partial(body, place))


SMEM = pl.BlockSpec(memory_space=pltpu.SMEM)
LIMIT = pltpu.CompilerParams(vmem_limit_bytes=16 * 1024 * 1024)


def attend(me, query, bounds, kv, packs, asked):
    packed = jax.ShapeDtypeStruct((8, 2 * HD), F32)
    return pl.pallas_call(
        attend_kernel,
        cost_estimate=COST,
        out_shape=(jax.ShapeDtypeStruct(query.shape, BF16), packed) + (packed,) * 4,
        in_specs=[SMEM] + [VMEM] * 12,
        out_specs=(VMEM,) * 6,
        scratch_shapes=[pltpu.VMEM((bounds.shape[0], kv[0].shape[1]), F32)],
        compiler_params=LIMIT,
    )(me, query, bounds, *kv, *packs, *asked)


def merge_kernel(flags_ref, attended_ref, own_ref, far_ref, mate_ref, perm_ref, keep_ref, give_ref):
    own = own_ref[...]
    far = jnp.where(flags_ref[1] == 1, far_ref[:4], mate_ref[4:])
    far = jnp.concatenate([far, far], 0)
    split = lambda packed: (
        packed[:, :HD], packed[:, HD : HD + 1], packed[:, 2 * HD - 1 : 2 * HD]
    )
    mixed_a, peak_a, total_a = split(own)
    mixed_b, peak_b, total_b = split(far)
    peak = jnp.maximum(peak_a, peak_b)
    scale_a = jnp.exp(peak_a - peak)
    scale_b = jnp.exp(peak_b - peak)
    ready = (mixed_a * scale_a + mixed_b * scale_b) / (total_a * scale_a + total_b * scale_b)
    ready = jnp.concatenate([ready[:STEPS], ready[STEPS : 2 * STEPS]], 1)
    attended = attended_ref[...]
    rows = attended.shape[0]
    lead = jnp.concatenate([ready] + [jnp.zeros_like(ready)] * (rows // STEPS - 1), 0)
    row = lax.broadcasted_iota(jnp.int32, lead.shape, 0)
    swap = (row < STEPS) & (flags_ref[0] == 1)
    attended = jnp.where(swap, lead, attended.astype(F32)).astype(BF16)
    attended = lax.dot_general(
        perm_ref[...], attended, (((0,), (0,)), ((), ())), preferred_element_type=F32
    ).astype(BF16)
    keep_ref[...] = attended[: rows // 2]
    give_ref[...] = attended[rows // 2 :]


def merge(flags, attended, own, far, mate, perm):
    rows, columns = attended.shape
    return pl.pallas_call(
        merge_kernel,
        cost_estimate=COST,
        out_shape=(jax.ShapeDtypeStruct((rows // 2, columns), BF16),) * 2,
        in_specs=[SMEM] + [VMEM] * 5,
        out_specs=(VMEM,) * 2,
    )(flags, attended, own, far, mate, perm)


def add_core_kernel(own_ref, across_ref, *out_refs):
    total = (own_ref[...].astype(F32) + across_ref[...].astype(F32)).astype(BF16)
    width = total.shape[0] // len(out_refs)
    for i, ref in enumerate(out_refs):
        ref[...] = total[i * width : (i + 1) * width]


def add_core(own, across):
    rows, columns = own.shape
    return pl.pallas_call(
        add_core_kernel,
        cost_estimate=COST,
        out_shape=(jax.ShapeDtypeStruct((rows // XN, columns), BF16),) * XN,
        in_specs=[VMEM, VMEM],
        out_specs=(VMEM,) * XN,
        compiler_params=LIMIT,
    )(own, across)


def add_x_kernel(a_ref, b_ref, c_ref, d_ref, own_ref, send_ref):
    total = a_ref[...].astype(F32)
    for ref in (b_ref, c_ref, d_ref):
        total = total + ref[...].astype(F32)
    half = total.shape[0] // 2
    own_ref[...] = total[:half]
    send_ref[...] = total[half:].astype(BF16)


def add_x(parts):
    rows, columns = parts[0].shape
    return pl.pallas_call(
        add_x_kernel,
        cost_estimate=COST,
        out_shape=(
            jax.ShapeDtypeStruct((rows // 2, columns), F32),
            jax.ShapeDtypeStruct((rows // 2, columns), BF16),
        ),
        in_specs=[VMEM] * 4,
        out_specs=(VMEM,) * 2,
    )(*parts)


def pick_row(table, selector):
    return jnp.sum(jnp.where(selector, table[None, :], 0), 1)


DISTANCES = ((3, 4), (-2, -3), (1, 2), (0, -1))


def carry(distances, groups, count, back):
    route = []
    for group in range(groups):
        for tp in range(count):
            far = (group + distances[tp % 2]) % groups
            asking = (groups + group) * count + tp
            asked = far * count + tp
            route.append((asked, asking) if back else (asking, asked))
    return route


def local(hidden, norm_gain, w_query, w_keyval, w_out, kv_cache, match, cache_lengths):
    side = lax.axis_index("role")
    group = lax.axis_index("grp")
    tp = lax.axis_index("tp")
    groups = lax.axis_size("grp")
    count = lax.axis_size("tp")
    own_rows = hidden[0, 0]
    block = own_rows.shape[0]
    row_count = block * count
    kv_t = kv_cache[0, 0].T
    cache_len = kv_t.shape[1]
    qcols = w_query.shape[1]
    kcols = w_keyval.shape[1]

    beside = lax.ppermute(own_rows, "tp", YHI)
    kv_y = lax.ppermute(kv_t, "tp", YHI)
    kv_core = lax.ppermute(kv_t, "tp", CORE)
    pair = norm(own_rows, beside, norm_gain)
    others = [lax.ppermute(pair, "tp", xshift(-k)) for k in range(1, XN)]
    w_query = fetch(after(w_query, pair))
    others = after(others, w_query, kv_core)
    own_half = jnp.concatenate([pair] + others, 0)
    mate_half = after(lax.ppermute(own_half, "tp", CORE), kv_y)
    kv_both = lax.ppermute(kv_y, "tp", CORE)

    slot = jnp.arange(row_count, dtype=jnp.int32)
    piece = slot // block
    far_core, far_x, far_y = piece // 8, piece // 2 % XN, piece % 2
    owner = (
        (tp // 4 + far_x) % XN * 4
        + jnp.bitwise_xor(tp // 2 % 2, far_y) * 2
        + jnp.bitwise_xor(tp % 2, far_core)
    )
    row_at = owner * block + slot % block
    row_ids = jnp.arange(row_count, dtype=jnp.int32)
    placed = row_at[None, :] == row_ids[:, None]
    perm = placed.astype(BF16)

    request = row_ids // STEPS
    step_ids = row_ids % STEPS
    lengths = cache_lengths[0]
    zero_one = jnp.zeros((1,), jnp.int32)
    bases = jnp.concatenate([jnp.full((1,), cache_len + row_count, jnp.int32), lengths])
    before = jnp.arange(lengths.shape[0])[None, :] < jnp.arange(lengths.shape[0])[:, None]
    offsets = pick_row(lengths, before)
    selector = request[:, None] == jnp.arange(row_count // STEPS, dtype=jnp.int32)[None, :]
    start = pick_row(jnp.concatenate([zero_one, offsets]), selector)
    span = pick_row(jnp.concatenate([zero_one, lengths]), selector)
    positions = jnp.where(side == 0, cache_len + row_ids, pick_row(bases, selector) + step_ids)
    low = jnp.where(side == 0, 0, start)
    high = jnp.where(side == 0, cache_len, start + span)
    fresh_low = jnp.where(side == 0, 0, request * STEPS)
    bounds = jnp.stack([low, high, fresh_low, row_ids], 1)
    whole = jnp.array([0, cache_len, 0, row_count - 1], jnp.int32)
    bounds = jnp.concatenate([bounds, bounds, jnp.broadcast_to(whole[None, :], (32, 4))], 0)

    position_at = jnp.sum(jnp.where(placed, positions[:, None], 0), 0).astype(F32)
    column = jnp.arange(qcols, dtype=jnp.int32)
    inverse = 500000.0 ** (-(2.0 / HD) * (column % HD // 2).astype(F32))
    angles = position_at[:, None] * inverse[None, :]
    cq = jnp.cos(angles)
    sq = jnp.sin(angles) * jnp.where(column % 2 == 0, -1.0, 1.0)[None, :]
    column = tp * kcols + jnp.arange(kcols, dtype=jnp.int32)
    inverse = 500000.0 ** (-(2.0 / HD) * (column % HD // 2).astype(F32))
    angles = inverse[:, None] * position_at[None, :]
    is_key = (column // HD % 2 == 0)[:, None]
    ck = jnp.where(is_key, jnp.cos(angles), 1.0)
    sk = jnp.where(is_key, jnp.sin(angles) * jnp.where(column % 2 == 0, -1.0, 1.0)[:, None], 0.0)

    query, pack = project(own_half, mate_half, w_query, w_keyval.T, cq, sq, ck, sk, perm)

    mate_pack = lax.ppermute(pack, "tp", CORE)
    packs = jnp.concatenate([pack, mate_pack], 0)
    leads = after(jnp.concatenate([pack[kcols:], mate_pack[kcols:]], 0), kv_both)
    axes = ("role", "grp", "tp")
    asked = [lax.ppermute(leads, axes, carry(d, groups, count, False)) for d in DISTANCES]
    packs = [packs, lax.ppermute(after(packs, leads), "tp", YHI)]
    kv = [kv_t, kv_core, kv_y, kv_both]
    me = jnp.reshape(tp % 4, (1,)).astype(jnp.int32)
    attended, lead_own, *answers = attend(me, query, bounds, kv, packs, asked)
    answers = [
        lax.ppermute(answer, axes, carry(d, groups, count, True))
        for answer, d in zip(answers, DISTANCES)
    ]

    far = jnp.zeros_like(answers[0])
    here = jnp.zeros((), jnp.bool_)
    for answer, pair_of in zip(answers, DISTANCES):
        distance = jnp.where(tp % 2 == 0, pair_of[0], pair_of[1])
        valid = jnp.sum(
            jnp.where(jnp.arange(groups) == (group + distance) % groups, match, 0)
        ) == group
        far = jnp.where(valid, answer, far)
        here = here | valid
    mate = lax.ppermute(far, "tp", CORE)
    flags = jnp.stack([side, here.astype(jnp.int32)])
    own_att, mate_att = merge(flags, attended, lead_own, far, mate, perm)

    give = jnp.dot(mate_att, w_out, preferred_element_type=F32).astype(BF16)
    across = lax.ppermute(give, "tp", CORE)
    keep = jnp.dot(own_att, w_out, preferred_element_type=F32).astype(BF16)
    parts = add_core(keep, across)
    parts = [parts[0]] + [lax.ppermute(parts[k], "tp", xshift(k)) for k in range(1, XN)]
    summed, send = add_x(parts)
    summed = summed + lax.ppermute(send, "tp", YHI).astype(F32)
    return (own_rows.astype(F32) + summed).astype(BF16)[None, None]


def solution(mesh):
    return jax.shard_map(
        local,
        mesh=mesh,
        in_specs=(
            P("role", "grp", "tp", None),
            P(),
            P(None, "tp"),
            P(None, "tp"),
            P("tp", None),
            P("role", "grp", None, "tp"),
            P(),
            P("grp", None),
        ),
        out_specs=P("role", "grp", "tp", None),
        check_vma=False,
    )
```

```python
import functools
import math

import jax
import jax.numpy as jnp
from jax import lax
from jax.experimental import pallas as pl
from jax.experimental.pallas import tpu as pltpu
from jax.sharding import PartitionSpec as P

HD = 128
STEPS = 2
XN = 4
NEG = -math.inf
F32 = jnp.float32
BF16 = jnp.bfloat16
VMEM = pl.BlockSpec(memory_space=pltpu.VMEM)
LIMIT = pltpu.CompilerParams(vmem_limit_bytes=8 * 1024 * 1024)
COST = pl.CostEstimate(flops=1, bytes_accessed=1, transcendentals=0)

CORE = [(i, i ^ 1) for i in range(16)]
YHI = [(i, i ^ 2) for i in range(16)]
BOTH = [(i, i ^ 3) for i in range(16)]


def xshift(k):
    return [(i, (i + 4 * k) % 16) for i in range(16)]


def after(value, *others):
    return lax.optimization_barrier((value,) + others)[0]


def norm_kernel(own_ref, beside_ref, gain_ref, out_ref):
    floated = jnp.concatenate([own_ref[...].astype(F32), beside_ref[...].astype(F32)], 0)
    spread = jnp.mean(floated * floated, axis=-1, keepdims=True)
    out_ref[...] = (floated * lax.rsqrt(spread + 1e-05) * gain_ref[...]).astype(BF16)


def norm(own, beside, gain):
    return pl.pallas_call(
        norm_kernel,
        cost_estimate=COST,
        compiler_params=LIMIT,
        out_shape=jax.ShapeDtypeStruct((2 * own.shape[0], own.shape[1]), BF16),
        in_specs=[VMEM, VMEM, VMEM],
        out_specs=VMEM,
    )(own, beside, gain[None, :])


def touch_kernel(*refs):
    refs[-1][...] = jnp.zeros(refs[-1].shape, F32)


def touch(*arrays):
    return pl.pallas_call(
        touch_kernel,
        cost_estimate=COST,
        compiler_params=LIMIT,
        out_shape=jax.ShapeDtypeStruct((8, HD), F32),
        in_specs=[VMEM] * len(arrays),
        out_specs=VMEM,
    )(*arrays)


def turn(value, cosine, sine, axis):
    size = value.shape[axis]
    index = lax.broadcasted_iota(jnp.int32, value.shape, axis)
    ahead = pltpu.roll(value, size - 1, axis)
    behind = pltpu.roll(value, 1, axis)
    return value * cosine + jnp.where(index % 2 == 0, ahead, behind) * sine


def project_kernel(
    own_ref, mate_ref, wq_ref, wkv_ref, cq_ref, sq_ref, ck_ref, sk_ref, perm_ref,
    token_ref, q_ref, pack_ref,
):
    del token_ref
    rows = jnp.concatenate([own_ref[...], mate_ref[...]], 0)
    query = jnp.dot(rows, wq_ref[...], preferred_element_type=F32)
    fresh = lax.dot_general(
        wkv_ref[...], rows, (((1,), (1,)), ((), ())), preferred_element_type=F32
    )
    perm = perm_ref[...]
    query = turn(query, cq_ref[...], sq_ref[...], 1).astype(BF16)
    query = jnp.dot(perm, query, preferred_element_type=F32)
    q_ref[...] = query.astype(BF16)
    fresh = turn(fresh, ck_ref[...], sk_ref[...], 0).astype(BF16)
    fresh = lax.dot_general(fresh, perm, (((1,), (1,)), ((), ())), preferred_element_type=F32)
    size = fresh.shape[0]
    pack_ref[:size, :] = jnp.concatenate([fresh, jnp.zeros_like(fresh)], 1).astype(BF16)
    lead = lead_rows(query[:, :HD], query[:, HD:])
    pack_ref[size:, :] = jnp.concatenate([lead, jnp.zeros_like(lead)], 0).astype(BF16)


def lead_rows(first, second):
    both = jnp.concatenate([first[:STEPS], second[:STEPS]], 0)
    return jnp.concatenate([both, jnp.zeros_like(both)], 0)


def project(own, mate, w_query, w_kv_t, cq, sq, ck, sk, perm, token):
    rows = 2 * own.shape[0]
    return pl.pallas_call(
        project_kernel,
        cost_estimate=COST,
        compiler_params=LIMIT,
        out_shape=(
            jax.ShapeDtypeStruct((rows, w_query.shape[1]), BF16),
            jax.ShapeDtypeStruct((w_kv_t.shape[0] + 16, HD), BF16),
        ),
        in_specs=[VMEM] * 10,
        out_specs=(VMEM,) * 2,
    )(own, mate, w_query, w_kv_t, cq, sq, ck, sk, perm, token)


def softmax_parts(queries, bounds, kv_refs, fresh, scores):
    tokens = kv_refs[0].shape[1]
    chunk = 512
    scale = 1.0 / math.sqrt(HD)
    if bounds is not None:
        low, high, fresh_low, fresh_high = bounds

    def pair(first, span):
        return jnp.concatenate([kv_refs[first][:, span], kv_refs[first + 1][:, span]], 0)

    fresh_keys = jnp.concatenate(fresh[:2], 0)
    fresh_values = jnp.concatenate(fresh[2:], 0)
    fresh_scores = jnp.dot(queries, fresh_keys, preferred_element_type=F32) * scale
    if bounds is not None:
        index = lax.broadcasted_iota(jnp.int32, fresh_scores.shape, 1)
        fresh_scores = jnp.where((index >= fresh_low) & (index <= fresh_high), fresh_scores, NEG)
    peak = jnp.max(fresh_scores, -1, keepdims=True)
    for start in range(0, tokens, chunk):
        span = slice(start, start + chunk)
        part_scores = jnp.dot(queries, pair(0, span), preferred_element_type=F32) * scale
        if bounds is not None:
            index = lax.broadcasted_iota(jnp.int32, part_scores.shape, 1) + start
            part_scores = jnp.where((index >= low) & (index < high), part_scores, NEG)
        scores[:, span] = part_scores
        peak = jnp.maximum(peak, jnp.max(part_scores, -1, keepdims=True))
    contract = (((1,), (1,)), ((), ()))
    weights = jnp.exp(fresh_scores - peak)
    total = jnp.sum(weights, -1, keepdims=True)
    mixed = lax.dot_general(
        weights.astype(BF16), fresh_values, contract, preferred_element_type=F32
    )
    for start in range(0, tokens, chunk):
        span = slice(start, start + chunk)
        weights = jnp.exp(scores[:, span] - peak)
        total += jnp.sum(weights, -1, keepdims=True)
        mixed += lax.dot_general(
            weights.astype(BF16), pair(2, span), contract, preferred_element_type=F32
        )
    return mixed, peak, total


def pack_parts(mixed, peak, total):
    lane = lax.broadcasted_iota(jnp.int32, mixed.shape, 1)
    return jnp.concatenate([mixed, jnp.where(lane < HD // 2, peak, total)], 1)


def in_order(place, held):
    return [held[place ^ part] for part in range(4)]


def each_place(me_ref, body):
    for place in range(4):
        pl.when(me_ref[0] == place)(functools.partial(body, place))


def held_fresh(pack_refs, size):
    return [ref[:size, :size] for ref in pack_refs]


def main_kernel(me_ref, q_ref, bounds_ref, w_ref, *refs):
    del w_ref
    kv_refs, pack_refs = refs[:4], refs[4:8]
    out_ref, lead_ref, scores = refs[8:]

    def body(place):
        query = q_ref[...]
        rows = query.shape[0]
        bounds = bounds_ref[...]
        mixed, peak, total = softmax_parts(
            jnp.concatenate([query[:, :HD], query[:, HD:]], 0),
            [bounds[:, i : i + 1] for i in range(4)],
            in_order(place, kv_refs),
            in_order(place, held_fresh(pack_refs, kv_refs[0].shape[0])),
            scores,
        )
        ready = mixed / total
        out_ref[...] = jnp.concatenate([ready[:rows], ready[rows:]], 1).astype(BF16)
        packed = pack_parts(mixed, peak, total)
        lead_ref[...] = lead_rows(packed[:8], packed[rows : rows + 8])

    each_place(me_ref, body)


def far_kernel(me_ref, *refs):
    kv_refs, pack_refs, asked = refs[:4], refs[4:8], refs[8:12]
    answers, scores = refs[12:16], refs[16]

    def body(place):
        far = []
        for ref in asked:
            both = ref[...].astype(F32)
            far += [both[:4], both[16:20]]
        mixed, peak, total = softmax_parts(
            jnp.concatenate(far, 0).astype(BF16),
            None,
            in_order(place, kv_refs),
            in_order(place, held_fresh(pack_refs, kv_refs[0].shape[0])),
            scores,
        )
        packed = pack_parts(mixed, peak, total)
        for i, ref in enumerate(answers):
            ref[...] = packed[8 * i : 8 * i + 8]

    each_place(me_ref, body)


SMEM = pl.BlockSpec(memory_space=pltpu.SMEM)


def attend_main(me, query, bounds, w_out, kv, packs):
    return pl.pallas_call(
        main_kernel,
        cost_estimate=COST,
        compiler_params=LIMIT,
        out_shape=(
            jax.ShapeDtypeStruct(query.shape, BF16),
            jax.ShapeDtypeStruct((8, 2 * HD), F32),
        ),
        in_specs=[SMEM] + [VMEM] * 11,
        out_specs=(VMEM,) * 2,
        scratch_shapes=[pltpu.VMEM((bounds.shape[0], kv[0].shape[1]), F32)],
    )(me, query, bounds, w_out, *kv, *packs)


def attend_far(me, kv, packs, asked):
    return pl.pallas_call(
        far_kernel,
        cost_estimate=COST,
        compiler_params=LIMIT,
        out_shape=(jax.ShapeDtypeStruct((8, 2 * HD), F32),) * 4,
        in_specs=[SMEM] + [VMEM] * 12,
        out_specs=(VMEM,) * 4,
        scratch_shapes=[pltpu.VMEM((32, kv[0].shape[1]), F32)],
    )(me, *kv, *packs, *asked)


def merge_kernel(flags_ref, attended_ref, own_ref, far_ref, mate_ref, perm_ref, w_ref, keep_ref, give_ref):
    own = own_ref[...]
    far = jnp.where(flags_ref[1] == 1, far_ref[:4], mate_ref[4:])
    far = jnp.concatenate([far, far], 0)
    split = lambda packed: (
        packed[:, :HD], packed[:, HD : HD + 1], packed[:, 2 * HD - 1 : 2 * HD]
    )
    mixed_a, peak_a, total_a = split(own)
    mixed_b, peak_b, total_b = split(far)
    peak = jnp.maximum(peak_a, peak_b)
    scale_a = jnp.exp(peak_a - peak)
    scale_b = jnp.exp(peak_b - peak)
    ready = (mixed_a * scale_a + mixed_b * scale_b) / (total_a * scale_a + total_b * scale_b)
    ready = jnp.concatenate([ready[:STEPS], ready[STEPS : 2 * STEPS]], 1)
    attended = attended_ref[...]
    rows = attended.shape[0]
    lead = jnp.concatenate([ready] + [jnp.zeros_like(ready)] * (rows // STEPS - 1), 0)
    row = lax.broadcasted_iota(jnp.int32, lead.shape, 0)
    swap = (row < STEPS) & (flags_ref[0] == 1)
    attended = jnp.where(swap, lead, attended.astype(F32)).astype(BF16)
    attended = lax.dot_general(
        perm_ref[...], attended, (((0,), (0,)), ((), ())), preferred_element_type=F32
    ).astype(BF16)
    width = 1024
    for first in range(0, w_ref.shape[1], width):
        span = slice(first, first + width)
        share = jnp.dot(attended, w_ref[:, span], preferred_element_type=F32).astype(BF16)
        keep_ref[:, span] = share[: rows // 2]
        give_ref[:, span] = share[rows // 2 :]


def merge(flags, attended, own, far, mate, perm, w_out):
    half = jax.ShapeDtypeStruct((attended.shape[0] // 2, w_out.shape[1]), BF16)
    return pl.pallas_call(
        merge_kernel,
        cost_estimate=COST,
        compiler_params=LIMIT,
        out_shape=(half, half),
        in_specs=[SMEM] + [VMEM] * 6,
        out_specs=(VMEM,) * 2,
    )(flags, attended, own, far, mate, perm, w_out)


def add_core_kernel(own_ref, across_ref, *out_refs):
    total = (own_ref[...].astype(F32) + across_ref[...].astype(F32)).astype(BF16)
    width = total.shape[0] // len(out_refs)
    for i, ref in enumerate(out_refs):
        ref[...] = total[i * width : (i + 1) * width]


def add_core(own, across):
    rows, columns = own.shape
    return pl.pallas_call(
        add_core_kernel,
        cost_estimate=COST,
        compiler_params=LIMIT,
        out_shape=(jax.ShapeDtypeStruct((rows // XN, columns), BF16),) * XN,
        in_specs=[VMEM, VMEM],
        out_specs=(VMEM,) * XN,
    )(own, across)


def add_x_kernel(a_ref, b_ref, c_ref, d_ref, own_ref, send_ref):
    total = a_ref[...].astype(F32)
    for ref in (b_ref, c_ref, d_ref):
        total = total + ref[...].astype(F32)
    half = total.shape[0] // 2
    own_ref[...] = total[:half]
    send_ref[...] = total[half:].astype(BF16)


def add_x(parts):
    rows, columns = parts[0].shape
    return pl.pallas_call(
        add_x_kernel,
        cost_estimate=COST,
        compiler_params=LIMIT,
        out_shape=(
            jax.ShapeDtypeStruct((rows // 2, columns), F32),
            jax.ShapeDtypeStruct((rows // 2, columns), BF16),
        ),
        in_specs=[VMEM] * 4,
        out_specs=(VMEM,) * 2,
    )(*parts)


def pick_row(table, selector):
    return jnp.sum(jnp.where(selector, table[None, :], 0), 1)


DISTANCES = ((0, -1), (1, 2), (-2, -3), (3, 4))


def carry(distances, groups, count, back):
    route = []
    for group in range(groups):
        for tp in range(count):
            far = (group + distances[tp % 2]) % groups
            asking = (groups + group) * count + tp
            asked = far * count + tp
            route.append((asked, asking) if back else (asking, asked))
    return route


def local(hidden, norm_gain, w_query, w_keyval, w_out, kv_cache, match, cache_lengths):
    side = lax.axis_index("role")
    group = lax.axis_index("grp")
    tp = lax.axis_index("tp")
    groups = lax.axis_size("grp")
    count = lax.axis_size("tp")
    own_rows = hidden[0, 0]
    block = own_rows.shape[0]
    row_count = block * count
    kv_t = kv_cache[0, 0].T
    cache_len = kv_t.shape[1]
    qcols = w_query.shape[1]
    kcols = w_keyval.shape[1]

    beside = lax.ppermute(own_rows, "tp", YHI)
    kv_sent = after(kv_t, beside)
    kv_y = lax.ppermute(kv_sent, "tp", YHI)
    kv_core = lax.ppermute(kv_sent, "tp", CORE)
    pair = norm(own_rows, beside, norm_gain)
    others = [lax.ppermute(pair, "tp", xshift(-k)) for k in range(1, XN)]
    token = touch(pair, w_query, w_keyval.T)
    others = after(others, kv_y, token)
    own_half = jnp.concatenate([pair] + others, 0)
    mate_half = after(lax.ppermute(own_half, "tp", CORE), kv_core)
    kv_both = lax.ppermute(kv_y, "tp", CORE)

    slot = jnp.arange(row_count, dtype=jnp.int32)
    piece = slot // block
    far_core, far_x, far_y = piece // 8, piece // 2 % XN, piece % 2
    owner = (
        (tp // 4 + far_x) % XN * 4
        + jnp.bitwise_xor(tp // 2 % 2, far_y) * 2
        + jnp.bitwise_xor(tp % 2, far_core)
    )
    row_at = owner * block + slot % block
    row_ids = jnp.arange(row_count, dtype=jnp.int32)
    placed = row_at[None, :] == row_ids[:, None]
    perm = placed.astype(BF16)

    request = row_ids // STEPS
    step_ids = row_ids % STEPS
    lengths = cache_lengths[0]
    zero_one = jnp.zeros((1,), jnp.int32)
    bases = jnp.concatenate([jnp.full((1,), cache_len + row_count, jnp.int32), lengths])
    before = jnp.arange(lengths.shape[0])[None, :] < jnp.arange(lengths.shape[0])[:, None]
    offsets = pick_row(lengths, before)
    selector = request[:, None] == jnp.arange(row_count // STEPS, dtype=jnp.int32)[None, :]
    start = pick_row(jnp.concatenate([zero_one, offsets]), selector)
    span = pick_row(jnp.concatenate([zero_one, lengths]), selector)
    positions = jnp.where(side == 0, cache_len + row_ids, pick_row(bases, selector) + step_ids)
    low = jnp.where(side == 0, 0, start)
    high = jnp.where(side == 0, cache_len, start + span)
    fresh_low = jnp.where(side == 0, 0, request * STEPS)
    bounds = jnp.stack([low, high, fresh_low, row_ids], 1)
    bounds = jnp.concatenate([bounds, bounds], 0)

    position_at = jnp.sum(jnp.where(placed, positions[:, None], 0), 0).astype(F32)
    column = jnp.arange(qcols, dtype=jnp.int32)
    inverse = 500000.0 ** (-(2.0 / HD) * (column % HD // 2).astype(F32))
    angles = position_at[:, None] * inverse[None, :]
    cq = jnp.cos(angles)
    sq = jnp.sin(angles) * jnp.where(column % 2 == 0, -1.0, 1.0)[None, :]
    column = tp * kcols + jnp.arange(kcols, dtype=jnp.int32)
    inverse = 500000.0 ** (-(2.0 / HD) * (column % HD // 2).astype(F32))
    angles = inverse[:, None] * position_at[None, :]
    is_key = (column // HD % 2 == 0)[:, None]
    ck = jnp.where(is_key, jnp.cos(angles), 1.0)
    sk = jnp.where(is_key, jnp.sin(angles) * jnp.where(column % 2 == 0, -1.0, 1.0)[:, None], 0.0)

    query, pack = project(own_half, mate_half, w_query, w_keyval.T, cq, sq, ck, sk, perm, token)

    y_pack = lax.ppermute(pack, "tp", YHI)
    mate_pack = lax.ppermute(pack, "tp", CORE)
    packs = [pack, mate_pack, y_pack, lax.ppermute(y_pack, "tp", CORE)]
    leads = after(jnp.concatenate([pack[kcols:], mate_pack[kcols:]], 0), kv_both)
    axes = ("role", "grp", "tp")
    asked = [lax.ppermute(leads, axes, carry(d, groups, count, False)) for d in DISTANCES]
    kv = [kv_t, kv_core, kv_y, kv_both]
    me = jnp.reshape(tp % 4, (1,)).astype(jnp.int32)
    answers = attend_far(me, kv, packs, asked)
    answers = [
        lax.ppermute(answer, axes, carry(d, groups, count, True))
        for answer, d in zip(answers, DISTANCES)
    ]
    query = after(query, asked)
    attended, lead_own = attend_main(me, query, bounds, w_out, kv, packs)

    answers = after(answers, attended)
    far = jnp.zeros_like(answers[0])
    here = jnp.zeros((), jnp.bool_)
    for answer, pair_of in zip(answers, DISTANCES):
        distance = jnp.where(tp % 2 == 0, pair_of[0], pair_of[1])
        valid = jnp.sum(
            jnp.where(jnp.arange(groups) == (group + distance) % groups, match, 0)
        ) == group
        far = jnp.where(valid, answer, far)
        here = here | valid
    mate = lax.ppermute(far, "tp", CORE)
    flags = jnp.stack([side, here.astype(jnp.int32)])
    keep, give = merge(flags, attended, lead_own, far, mate, perm, w_out)

    across = lax.ppermute(give, "tp", CORE)
    parts = add_core(keep, across)
    parts = [parts[0]] + [lax.ppermute(parts[k], "tp", xshift(k)) for k in range(1, XN)]
    summed, send = add_x(parts)
    summed = summed + lax.ppermute(send, "tp", YHI).astype(F32)
    return (own_rows.astype(F32) + summed).astype(BF16)[None, None]


def solution(mesh):
    return jax.shard_map(
        local,
        mesh=mesh,
        in_specs=(
            P("role", "grp", "tp", None),
            P(),
            P(None, "tp"),
            P(None, "tp"),
            P("tp", None),
            P("role", "grp", None, "tp"),
            P(),
            P("grp", None),
        ),
        out_specs=P("role", "grp", "tp", None),
        check_vma=False,
    )
```

```python
import functools
import math

import jax
import jax.numpy as jnp
from jax import lax
from jax.experimental import pallas as pl
from jax.experimental.pallas import tpu as pltpu
from jax.sharding import PartitionSpec as P

HD = 128
STEPS = 2
XN = 4
NEG = -math.inf
F32 = jnp.float32
BF16 = jnp.bfloat16
VMEM = pl.BlockSpec(memory_space=pltpu.VMEM)
LIMIT = pltpu.CompilerParams(vmem_limit_bytes=8 * 1024 * 1024)
COST = pl.CostEstimate(flops=1, bytes_accessed=1, transcendentals=0)

CORE = [(i, i ^ 1) for i in range(16)]
YHI = [(i, i ^ 2) for i in range(16)]
BOTH = [(i, i ^ 3) for i in range(16)]


def xshift(k):
    return [(i, (i + 4 * k) % 16) for i in range(16)]


DISTANCES = ((0, -1), (1, 2), (-2, -3), (3, 4))


def after(value, *others):
    return lax.optimization_barrier((value,) + others)[0]


def scaled(rows, gain):
    floated = rows.astype(F32)
    spread = jnp.mean(floated * floated, axis=-1, keepdims=True)
    return floated * lax.rsqrt(spread + 1e-05) * gain


def stage_kernel(own_ref, gain_ref, out_ref, kept_ref):
    out_ref[...] = scaled(own_ref[...], gain_ref[...])
    kept_ref[...] = gain_ref[...]


def norm_kernel(own_ref, gain_ref, beside_ref, out_ref):
    beside = scaled(beside_ref[...], gain_ref[...])
    out_ref[...] = jnp.concatenate([own_ref[...], beside], 0).astype(BF16)


def stage(own, gain):
    return pl.pallas_call(
        stage_kernel,
        cost_estimate=COST,
        compiler_params=LIMIT,
        out_shape=(
            jax.ShapeDtypeStruct(own.shape, F32),
            jax.ShapeDtypeStruct(gain.shape, F32),
        ),
        in_specs=[VMEM] * 2,
        out_specs=(VMEM,) * 2,
    )(own, gain)


def norm(own, gain, beside):
    return pl.pallas_call(
        norm_kernel,
        cost_estimate=COST,
        compiler_params=LIMIT,
        out_shape=jax.ShapeDtypeStruct((2 * own.shape[0], own.shape[1]), BF16),
        in_specs=[VMEM] * 3,
        out_specs=VMEM,
    )(own, gain, beside)


def touch_kernel(*refs):
    refs[-1][...] = jnp.zeros(refs[-1].shape, F32)


def touch(*arrays):
    return pl.pallas_call(
        touch_kernel,
        cost_estimate=COST,
        compiler_params=LIMIT,
        out_shape=jax.ShapeDtypeStruct((8, HD), F32),
        in_specs=[VMEM] * len(arrays),
        out_specs=VMEM,
    )(*arrays)


def turn(value, cosine, sine, axis):
    size = value.shape[axis]
    index = lax.broadcasted_iota(jnp.int32, value.shape, axis)
    ahead = pltpu.roll(value, size - 1, axis)
    behind = pltpu.roll(value, 1, axis)
    return value * cosine + jnp.where(index % 2 == 0, ahead, behind) * sine


def project_kernel(
    own_ref, mate_ref, wq_ref, wkv_ref, cq_ref, sq_ref, ck_ref, sk_ref, perm_ref,
    token_ref, q_ref, pack_ref,
):
    del token_ref
    rows = jnp.concatenate([own_ref[...], mate_ref[...]], 0)
    query = jnp.dot(rows, wq_ref[...], preferred_element_type=F32)
    fresh = lax.dot_general(
        wkv_ref[...], rows, (((1,), (1,)), ((), ())), preferred_element_type=F32
    )
    perm = perm_ref[...]
    query = turn(query, cq_ref[...], sq_ref[...], 1).astype(BF16)
    query = jnp.dot(perm, query, preferred_element_type=F32)
    q_ref[...] = query.astype(BF16)
    fresh = turn(fresh, ck_ref[...], sk_ref[...], 0).astype(BF16)
    fresh = lax.dot_general(fresh, perm, (((1,), (1,)), ((), ())), preferred_element_type=F32)
    size = fresh.shape[0]
    pack_ref[:size, :] = jnp.concatenate([fresh, jnp.zeros_like(fresh)], 1).astype(BF16)
    lead = lead_rows(query[:, :HD], query[:, HD:])
    pack_ref[size:, :] = jnp.concatenate([lead, jnp.zeros_like(lead)], 0).astype(BF16)


def lead_rows(first, second):
    both = jnp.concatenate([first[:STEPS], second[:STEPS]], 0)
    return jnp.concatenate([both, jnp.zeros_like(both)], 0)


def project(own, mate, w_query, w_kv_t, cq, sq, ck, sk, perm, token):
    rows = 2 * own.shape[0]
    return pl.pallas_call(
        project_kernel,
        cost_estimate=COST,
        compiler_params=LIMIT,
        out_shape=(
            jax.ShapeDtypeStruct((rows, w_query.shape[1]), BF16),
            jax.ShapeDtypeStruct((w_kv_t.shape[0] + 16, HD), BF16),
        ),
        in_specs=[VMEM] * 10,
        out_specs=(VMEM,) * 2,
    )(own, mate, w_query, w_kv_t, cq, sq, ck, sk, perm, token)


def softmax_parts(queries, bounds, kv_refs, fresh, scores):
    tokens = kv_refs[0].shape[1]
    chunk = 512
    scale = 1.0 / math.sqrt(HD)
    if bounds is not None:
        low, high, fresh_low, fresh_high = bounds

    def pair(first, span):
        return jnp.concatenate([kv_refs[first][:, span], kv_refs[first + 1][:, span]], 0)

    fresh_keys = jnp.concatenate(fresh[:2], 0)
    fresh_values = jnp.concatenate(fresh[2:], 0)
    fresh_scores = jnp.dot(queries, fresh_keys, preferred_element_type=F32) * scale
    if bounds is not None:
        index = lax.broadcasted_iota(jnp.int32, fresh_scores.shape, 1)
        fresh_scores = jnp.where((index >= fresh_low) & (index <= fresh_high), fresh_scores, NEG)
    peak = jnp.max(fresh_scores, -1, keepdims=True)
    for start in range(0, tokens, chunk):
        span = slice(start, start + chunk)
        part_scores = jnp.dot(queries, pair(0, span), preferred_element_type=F32) * scale
        if bounds is not None:
            index = lax.broadcasted_iota(jnp.int32, part_scores.shape, 1) + start
            part_scores = jnp.where((index >= low) & (index < high), part_scores, NEG)
        scores[:, span] = part_scores
        peak = jnp.maximum(peak, jnp.max(part_scores, -1, keepdims=True))
    contract = (((1,), (1,)), ((), ()))
    weights = jnp.exp(fresh_scores - peak)
    total = jnp.sum(weights, -1, keepdims=True)
    mixed = lax.dot_general(
        weights.astype(BF16), fresh_values, contract, preferred_element_type=F32
    )
    for start in range(0, tokens, chunk):
        span = slice(start, start + chunk)
        weights = jnp.exp(scores[:, span] - peak)
        total += jnp.sum(weights, -1, keepdims=True)
        mixed += lax.dot_general(
            weights.astype(BF16), pair(2, span), contract, preferred_element_type=F32
        )
    return mixed, peak, total


def pack_parts(mixed, peak, total):
    lane = lax.broadcasted_iota(jnp.int32, mixed.shape, 1)
    return jnp.concatenate([mixed, jnp.where(lane < HD // 2, peak, total)], 1)


def in_order(place, held):
    return [held[place ^ part] for part in range(4)]


def each_place(me_ref, body):
    for place in range(4):
        pl.when(me_ref[0] == place)(functools.partial(body, place))


def held_fresh(pack_refs, size):
    return [ref[:size, :size] for ref in pack_refs]


def main_kernel(me_ref, q_ref, bounds_ref, w_ref, *refs):
    del w_ref
    kv_refs, pack_refs = refs[:4], refs[4:8]
    out_ref, lead_ref, scores = refs[8:]

    def body(place):
        query = q_ref[...]
        rows = query.shape[0]
        bounds = bounds_ref[...]
        mixed, peak, total = softmax_parts(
            jnp.concatenate([query[:, :HD], query[:, HD:]], 0),
            [bounds[:, i : i + 1] for i in range(4)],
            in_order(place, kv_refs),
            in_order(place, held_fresh(pack_refs, kv_refs[0].shape[0])),
            scores,
        )
        ready = mixed / total
        out_ref[...] = jnp.concatenate([ready[:rows], ready[rows:]], 1).astype(BF16)
        packed = pack_parts(mixed, peak, total)
        lead_ref[...] = lead_rows(packed[:8], packed[rows : rows + 8])

    each_place(me_ref, body)


def far_kernel(me_ref, *refs):
    kv_refs, pack_refs, asked = refs[:4], refs[4:8], refs[8:12]
    answers, scores = refs[12:16], refs[16]

    def body(place):
        far = []
        for ref in asked:
            both = ref[...].astype(F32)
            far += [both[:4], both[16:20]]
        mixed, peak, total = softmax_parts(
            jnp.concatenate(far, 0).astype(BF16),
            None,
            in_order(place, kv_refs),
            in_order(place, held_fresh(pack_refs, kv_refs[0].shape[0])),
            scores,
        )
        packed = pack_parts(mixed, peak, total)
        for i, ref in enumerate(answers):
            ref[...] = packed[8 * i : 8 * i + 8]

    each_place(me_ref, body)


SMEM = pl.BlockSpec(memory_space=pltpu.SMEM)


def attend_main(me, query, bounds, w_out, kv, packs):
    return pl.pallas_call(
        main_kernel,
        cost_estimate=COST,
        compiler_params=LIMIT,
        out_shape=(
            jax.ShapeDtypeStruct(query.shape, BF16),
            jax.ShapeDtypeStruct((8, 2 * HD), F32),
        ),
        in_specs=[SMEM] + [VMEM] * 11,
        out_specs=(VMEM,) * 2,
        scratch_shapes=[pltpu.VMEM((bounds.shape[0], kv[0].shape[1]), F32)],
    )(me, query, bounds, w_out, *kv, *packs)


def attend_far(me, kv, packs, asked):
    return pl.pallas_call(
        far_kernel,
        cost_estimate=COST,
        compiler_params=LIMIT,
        out_shape=(jax.ShapeDtypeStruct((8, 2 * HD), F32),) * 4,
        in_specs=[SMEM] + [VMEM] * 12,
        out_specs=(VMEM,) * 4,
        scratch_shapes=[pltpu.VMEM((32, kv[0].shape[1]), F32)],
    )(me, *kv, *packs, *asked)


def distance_of(flags_ref, distances):
    return jnp.where(flags_ref[2] == 0, distances[0], distances[1])


def pick_kernel(flags_ref, match_ref, *refs):
    far = jnp.zeros(refs[-1].shape, F32)
    group, groups = flags_ref[1], match_ref.shape[0]
    for ref, distances in zip(refs, DISTANCES):
        prompt = lax.rem(group + distance_of(flags_ref, distances) + groups, groups)
        far = jnp.where(match_ref[prompt] == group, ref[...], far)
    refs[-1][...] = far


def pick(flags, match, answers):
    return pl.pallas_call(
        pick_kernel,
        cost_estimate=COST,
        compiler_params=LIMIT,
        out_shape=jax.ShapeDtypeStruct(answers[0].shape, F32),
        in_specs=[SMEM] * 2 + [VMEM] * len(answers),
        out_specs=VMEM,
    )(flags, match, *answers)


def merge_kernel(flags_ref, attended_ref, own_ref, far_ref, mate_ref, perm_ref, w_ref, keep_ref, give_ref):
    own = own_ref[...]
    far = far_ref[:4] + mate_ref[4:]
    far = jnp.concatenate([far, far], 0)
    split = lambda packed: (
        packed[:, :HD], packed[:, HD : HD + 1], packed[:, 2 * HD - 1 : 2 * HD]
    )
    mixed_a, peak_a, total_a = split(own)
    mixed_b, peak_b, total_b = split(far)
    peak = jnp.maximum(peak_a, peak_b)
    scale_a = jnp.exp(peak_a - peak)
    scale_b = jnp.exp(peak_b - peak)
    ready = (mixed_a * scale_a + mixed_b * scale_b) / (total_a * scale_a + total_b * scale_b)
    ready = jnp.concatenate([ready[:STEPS], ready[STEPS : 2 * STEPS]], 1)
    attended = attended_ref[...]
    rows = attended.shape[0]
    lead = jnp.concatenate([ready] + [jnp.zeros_like(ready)] * (rows // STEPS - 1), 0)
    row = lax.broadcasted_iota(jnp.int32, lead.shape, 0)
    swap = (row < STEPS) & (flags_ref[0] == 1)
    attended = jnp.where(swap, lead, attended.astype(F32)).astype(BF16)
    attended = lax.dot_general(
        perm_ref[...], attended, (((0,), (0,)), ((), ())), preferred_element_type=F32
    ).astype(BF16)
    keep_ref[...] = attended[: rows // 2]
    shares_kernel_body(attended[rows // 2 :], w_ref, give_ref)


def shares_kernel_body(attended, w_ref, out_ref):
    width = 1024
    for first in range(0, w_ref.shape[1], width):
        span = slice(first, first + width)
        out_ref[:, span] = jnp.dot(attended, w_ref[:, span], preferred_element_type=F32).astype(BF16)


def shares_kernel(attended_ref, w_ref, out_ref):
    shares_kernel_body(attended_ref[...], w_ref, out_ref)


def shares(attended, w_out):
    return pl.pallas_call(
        shares_kernel,
        cost_estimate=COST,
        compiler_params=LIMIT,
        out_shape=jax.ShapeDtypeStruct((attended.shape[0], w_out.shape[1]), BF16),
        in_specs=[VMEM] * 2,
        out_specs=VMEM,
    )(attended, w_out)


def merge(flags, attended, own, far, mate, perm, w_out):
    half = jax.ShapeDtypeStruct((attended.shape[0] // 2, w_out.shape[1]), BF16)
    return pl.pallas_call(
        merge_kernel,
        cost_estimate=COST,
        compiler_params=LIMIT,
        out_shape=(jax.ShapeDtypeStruct((half.shape[0], attended.shape[1]), BF16), half),
        in_specs=[SMEM] + [VMEM] * 6,
        out_specs=(VMEM,) * 2,
    )(flags, attended, own, far, mate, perm, w_out)


def add_core_kernel(own_ref, across_ref, *out_refs):
    total = (own_ref[...].astype(F32) + across_ref[...].astype(F32)).astype(BF16)
    width = total.shape[0] // len(out_refs)
    for i, ref in enumerate(out_refs):
        ref[...] = total[i * width : (i + 1) * width]


def add_core(own, across):
    rows, columns = own.shape
    return pl.pallas_call(
        add_core_kernel,
        cost_estimate=COST,
        compiler_params=LIMIT,
        out_shape=(jax.ShapeDtypeStruct((rows // XN, columns), BF16),) * XN,
        in_specs=[VMEM, VMEM],
        out_specs=(VMEM,) * XN,
    )(own, across)


def add_x_kernel(a_ref, b_ref, c_ref, d_ref, own_ref, send_ref):
    total = a_ref[...].astype(F32)
    for ref in (b_ref, c_ref, d_ref):
        total = total + ref[...].astype(F32)
    half = total.shape[0] // 2
    own_ref[...] = total[:half]
    send_ref[...] = total[half:].astype(BF16)


def add_x(parts):
    rows, columns = parts[0].shape
    return pl.pallas_call(
        add_x_kernel,
        cost_estimate=COST,
        compiler_params=LIMIT,
        out_shape=(
            jax.ShapeDtypeStruct((rows // 2, columns), F32),
            jax.ShapeDtypeStruct((rows // 2, columns), BF16),
        ),
        in_specs=[VMEM] * 4,
        out_specs=(VMEM,) * 2,
    )(*parts)


def pick_row(table, selector):
    return jnp.sum(jnp.where(selector, table[None, :], 0), 1)


def carry(distances, groups, count, back):
    route = []
    for group in range(groups):
        for tp in range(count):
            far = (group + distances[tp % 2]) % groups
            asking = (groups + group) * count + tp
            asked = far * count + tp
            route.append((asked, asking) if back else (asking, asked))
    return route


def local(hidden, norm_gain, w_query, w_keyval, w_out, kv_cache, match, cache_lengths):
    side = lax.axis_index("role")
    group = lax.axis_index("grp")
    tp = lax.axis_index("tp")
    groups = lax.axis_size("grp")
    count = lax.axis_size("tp")
    own_rows = hidden[0, 0]
    block = own_rows.shape[0]
    row_count = block * count
    kv_t = kv_cache[0, 0].T
    cache_len = kv_t.shape[1]
    qcols = w_query.shape[1]
    kcols = w_keyval.shape[1]

    beside = lax.ppermute(own_rows, "tp", YHI)
    staged = stage(own_rows, norm_gain[None, :])
    beside = after(beside, staged)
    kv_sent = after(kv_t, staged)
    kv_y = lax.ppermute(kv_sent, "tp", YHI)
    kv_core = lax.ppermute(kv_sent, "tp", CORE)
    pair = norm(*staged, beside)
    others = [lax.ppermute(pair, "tp", xshift(-k)) for k in range(1, XN)]
    token = touch(pair, w_query, w_keyval.T)
    others = after(others, kv_y, token)
    own_half = jnp.concatenate([pair] + others, 0)
    mate_half = after(lax.ppermute(own_half, "tp", CORE), kv_core)
    kv_both = lax.ppermute(kv_y, "tp", CORE)

    slot = jnp.arange(row_count, dtype=jnp.int32)
    piece = slot // block
    far_core, far_x, far_y = piece // 8, piece // 2 % XN, piece % 2
    owner = (
        (tp // 4 + far_x) % XN * 4
        + jnp.bitwise_xor(tp // 2 % 2, far_y) * 2
        + jnp.bitwise_xor(tp % 2, far_core)
    )
    row_at = owner * block + slot % block
    row_ids = jnp.arange(row_count, dtype=jnp.int32)
    placed = row_at[None, :] == row_ids[:, None]
    perm = placed.astype(BF16)

    request = row_ids // STEPS
    step_ids = row_ids % STEPS
    lengths = after(cache_lengths[0], pair)
    zero_one = jnp.zeros((1,), jnp.int32)
    bases = jnp.concatenate([jnp.full((1,), cache_len + row_count, jnp.int32), lengths])
    before = jnp.arange(lengths.shape[0])[None, :] < jnp.arange(lengths.shape[0])[:, None]
    offsets = pick_row(lengths, before)
    selector = request[:, None] == jnp.arange(row_count // STEPS, dtype=jnp.int32)[None, :]
    start = pick_row(jnp.concatenate([zero_one, offsets]), selector)
    span = pick_row(jnp.concatenate([zero_one, lengths]), selector)
    positions = jnp.where(side == 0, cache_len + row_ids, pick_row(bases, selector) + step_ids)
    low = jnp.where(side == 0, 0, start)
    high = jnp.where(side == 0, cache_len, start + span)
    fresh_low = jnp.where(side == 0, 0, request * STEPS)
    bounds = jnp.stack([low, high, fresh_low, row_ids], 1)
    bounds = jnp.concatenate([bounds, bounds], 0)

    position_at = jnp.sum(jnp.where(placed, positions[:, None], 0), 0).astype(F32)
    column = jnp.arange(qcols, dtype=jnp.int32)
    inverse = 500000.0 ** (-(2.0 / HD) * (column % HD // 2).astype(F32))
    angles = position_at[:, None] * inverse[None, :]
    cq = jnp.cos(angles)
    sq = jnp.sin(angles) * jnp.where(column % 2 == 0, -1.0, 1.0)[None, :]
    column = tp * kcols + jnp.arange(kcols, dtype=jnp.int32)
    inverse = 500000.0 ** (-(2.0 / HD) * (column % HD // 2).astype(F32))
    angles = inverse[:, None] * position_at[None, :]
    is_key = (column // HD % 2 == 0)[:, None]
    ck = jnp.where(is_key, jnp.cos(angles), 1.0)
    sk = jnp.where(is_key, jnp.sin(angles) * jnp.where(column % 2 == 0, -1.0, 1.0)[:, None], 0.0)

    query, pack = project(own_half, mate_half, w_query, w_keyval.T, cq, sq, ck, sk, perm, token)

    y_pack = lax.ppermute(pack, "tp", YHI)
    mate_pack = lax.ppermute(pack, "tp", CORE)
    packs = [pack, mate_pack, y_pack, lax.ppermute(y_pack, "tp", CORE)]
    leads = after(jnp.concatenate([pack[kcols:], mate_pack[kcols:]], 0), kv_both)
    axes = ("role", "grp", "tp")
    asked = [lax.ppermute(leads, axes, carry(d, groups, count, False)) for d in DISTANCES]
    kv = [kv_t, kv_core, kv_y, kv_both]
    me = jnp.reshape(tp % 4, (1,)).astype(jnp.int32)
    flags = jnp.stack([side, group, tp % 2]).astype(jnp.int32)
    answers = attend_far(me, kv, packs, asked)
    answers = [
        lax.ppermute(answer, axes, carry(d, groups, count, True))
        for answer, d in zip(answers, DISTANCES)
    ]
    query = after(query, asked)
    attended, lead_own = attend_main(me, query, bounds, w_out, kv, packs)

    answers = after(answers, attended)
    far = pick(flags, match, answers)
    mate = lax.ppermute(far, "tp", CORE)
    keep, give = merge(flags, attended, lead_own, far, mate, perm, w_out)

    across = lax.ppermute(give, "tp", CORE)
    keep = shares(keep, w_out)
    parts = add_core(keep, across)
    parts = [parts[0]] + [lax.ppermute(parts[k], "tp", xshift(k)) for k in range(1, XN)]
    summed, send = add_x(parts)
    summed = summed + lax.ppermute(send, "tp", YHI).astype(F32)
    return (own_rows.astype(F32) + summed).astype(BF16)[None, None]


def solution(mesh):
    return jax.shard_map(
        local,
        mesh=mesh,
        in_specs=(
            P("role", "grp", "tp", None),
            P(),
            P(None, "tp"),
            P(None, "tp"),
            P("tp", None),
            P("role", "grp", None, "tp"),
            P(),
            P("grp", None),
        ),
        out_specs=P("role", "grp", "tp", None),
        check_vma=False,
    )
```

```python
import functools
import math

import jax
import jax.numpy as jnp
from jax import lax
from jax.experimental import pallas as pl
from jax.experimental.pallas import tpu as pltpu
from jax.sharding import PartitionSpec as P

HD = 128
STEPS = 2
XN = 4
X_ORDER = (2, 1, 3)
NEG = -math.inf
F32 = jnp.float32
BF16 = jnp.bfloat16
VMEM = pl.BlockSpec(memory_space=pltpu.VMEM)
LIMIT = pltpu.CompilerParams(vmem_limit_bytes=8 * 1024 * 1024)
COST = pl.CostEstimate(flops=1, bytes_accessed=1, transcendentals=0)

CORE = [(i, i ^ 1) for i in range(16)]
YHI = [(i, i ^ 2) for i in range(16)]
BOTH = [(i, i ^ 3) for i in range(16)]


def xshift(k):
    return [(i, (i + 4 * k) % 16) for i in range(16)]


DISTANCES = ((3, 4), (-2, -3), (1, 2), (0, -1))


def after(value, *others):
    return lax.optimization_barrier((value,) + others)[0]


def scaled(rows):
    floated = rows.astype(F32)
    spread = jnp.mean(floated * floated, axis=-1, keepdims=True)
    return floated * lax.rsqrt(spread + 1e-05)


def stage_kernel(own_ref, out_ref):
    out_ref[...] = scaled(own_ref[...])


def keep_kernel(gain_ref, kept_ref):
    kept_ref[...] = gain_ref[...]


def norm_kernel(own_ref, gain_ref, beside_ref, out_ref):
    both = jnp.concatenate([own_ref[...], scaled(beside_ref[...])], 0)
    out_ref[...] = (both * gain_ref[...]).astype(BF16)


def stage(kernel, value):
    return pl.pallas_call(
        kernel,
        cost_estimate=COST,
        compiler_params=LIMIT,
        out_shape=jax.ShapeDtypeStruct(value.shape, F32),
        in_specs=[VMEM],
        out_specs=VMEM,
    )(value)


def norm(own, gain, beside):
    return pl.pallas_call(
        norm_kernel,
        cost_estimate=COST,
        compiler_params=LIMIT,
        out_shape=jax.ShapeDtypeStruct((2 * own.shape[0], own.shape[1]), BF16),
        in_specs=[VMEM] * 3,
        out_specs=VMEM,
    )(own, gain, beside)


def touch_kernel(*refs):
    refs[-1][...] = jnp.zeros(refs[-1].shape, F32)


def touch(*arrays):
    return pl.pallas_call(
        touch_kernel,
        cost_estimate=COST,
        compiler_params=LIMIT,
        out_shape=jax.ShapeDtypeStruct((8, HD), F32),
        in_specs=[VMEM] * len(arrays),
        out_specs=VMEM,
    )(*arrays)


def turn(value, cosine, sine, axis):
    size = value.shape[axis]
    index = lax.broadcasted_iota(jnp.int32, value.shape, axis)
    ahead = pltpu.roll(value, size - 1, axis)
    behind = pltpu.roll(value, 1, axis)
    return value * cosine + jnp.where(index % 2 == 0, ahead, behind) * sine


def project_kernel(
    own_ref, mate_ref, wq_ref, wkv_ref, cq_ref, sq_ref, ck_ref, sk_ref, perm_ref,
    token_ref, q_ref, pack_ref,
):
    del token_ref
    rows = jnp.concatenate([own_ref[...], mate_ref[...]], 0)
    query = jnp.dot(rows, wq_ref[...], preferred_element_type=F32)
    fresh = lax.dot_general(
        wkv_ref[...], rows, (((1,), (1,)), ((), ())), preferred_element_type=F32
    )
    perm = perm_ref[...]
    query = turn(query, cq_ref[...], sq_ref[...], 1).astype(BF16)
    query = jnp.dot(perm, query, preferred_element_type=F32)
    q_ref[...] = query.astype(BF16)
    fresh = turn(fresh, ck_ref[...], sk_ref[...], 0).astype(BF16)
    fresh = lax.dot_general(fresh, perm, (((1,), (1,)), ((), ())), preferred_element_type=F32)
    size = fresh.shape[0]
    pack_ref[:size, :] = jnp.concatenate([fresh, jnp.zeros_like(fresh)], 1).astype(BF16)
    lead = lead_rows(query[:, :HD], query[:, HD:])
    pack_ref[size:, :] = jnp.concatenate([lead, jnp.zeros_like(lead)], 0).astype(BF16)


def lead_rows(first, second):
    both = jnp.concatenate([first[:STEPS], second[:STEPS]], 0)
    return jnp.concatenate([both, jnp.zeros_like(both)], 0)


def project(own, mate, w_query, w_kv_t, cq, sq, ck, sk, perm, token):
    rows = 2 * own.shape[0]
    return pl.pallas_call(
        project_kernel,
        cost_estimate=COST,
        compiler_params=LIMIT,
        out_shape=(
            jax.ShapeDtypeStruct((rows, w_query.shape[1]), BF16),
            jax.ShapeDtypeStruct((w_kv_t.shape[0] + 16, HD), BF16),
        ),
        in_specs=[VMEM] * 10,
        out_specs=(VMEM,) * 2,
    )(own, mate, w_query, w_kv_t, cq, sq, ck, sk, perm, token)


def softmax_parts(queries, bounds, kv_refs, fresh, scores):
    tokens = kv_refs[0].shape[1]
    chunk = 512
    scale = 1.0 / math.sqrt(HD)
    if bounds is not None:
        low, high, fresh_low, fresh_high = bounds

    def pair(first, span):
        return jnp.concatenate([kv_refs[first][:, span], kv_refs[first + 1][:, span]], 0)

    fresh_keys = jnp.concatenate(fresh[:2], 0)
    fresh_values = jnp.concatenate(fresh[2:], 0)
    fresh_scores = jnp.dot(queries, fresh_keys, preferred_element_type=F32) * scale
    if bounds is not None:
        index = lax.broadcasted_iota(jnp.int32, fresh_scores.shape, 1)
        fresh_scores = jnp.where((index >= fresh_low) & (index <= fresh_high), fresh_scores, NEG)
    peak = jnp.max(fresh_scores, -1, keepdims=True)
    for start in range(0, tokens, chunk):
        span = slice(start, start + chunk)
        part_scores = jnp.dot(queries, pair(0, span), preferred_element_type=F32) * scale
        if bounds is not None:
            index = lax.broadcasted_iota(jnp.int32, part_scores.shape, 1) + start
            part_scores = jnp.where((index >= low) & (index < high), part_scores, NEG)
        scores[:, span] = part_scores
        peak = jnp.maximum(peak, jnp.max(part_scores, -1, keepdims=True))
    contract = (((1,), (1,)), ((), ()))
    weights = jnp.exp(fresh_scores - peak)
    total = jnp.sum(weights, -1, keepdims=True)
    mixed = lax.dot_general(
        weights.astype(BF16), fresh_values, contract, preferred_element_type=F32
    )
    for start in range(0, tokens, chunk):
        span = slice(start, start + chunk)
        weights = jnp.exp(scores[:, span] - peak)
        total += jnp.sum(weights, -1, keepdims=True)
        mixed += lax.dot_general(
            weights.astype(BF16), pair(2, span), contract, preferred_element_type=F32
        )
    return mixed, peak, total


def pack_parts(mixed, peak, total):
    lane = lax.broadcasted_iota(jnp.int32, mixed.shape, 1)
    return jnp.concatenate([mixed, jnp.where(lane < HD // 2, peak, total)], 1)


def in_order(place, held):
    return [held[place ^ part] for part in range(4)]


def each_place(me_ref, body):
    for place in range(4):
        pl.when(me_ref[0] == place)(functools.partial(body, place))


def held_fresh(pack_refs, size):
    return [ref[:size, :size] for ref in pack_refs]


def main_kernel(me_ref, q_ref, bounds_ref, w_ref, *refs):
    del w_ref
    kv_refs, pack_refs = refs[:4], refs[4:8]
    out_ref, lead_ref, scores = refs[8:]

    def body(place):
        query = q_ref[...]
        rows = query.shape[0]
        bounds = bounds_ref[...]
        mixed, peak, total = softmax_parts(
            jnp.concatenate([query[:, :HD], query[:, HD:]], 0),
            [bounds[:, i : i + 1] for i in range(4)],
            in_order(place, kv_refs),
            in_order(place, held_fresh(pack_refs, kv_refs[0].shape[0])),
            scores,
        )
        ready = mixed / total
        out_ref[...] = jnp.concatenate([ready[:rows], ready[rows:]], 1).astype(BF16)
        packed = pack_parts(mixed, peak, total)
        lead_ref[...] = lead_rows(packed[:8], packed[rows : rows + 8])

    each_place(me_ref, body)


def far_kernel(me_ref, *refs):
    kv_refs, pack_refs, asked = refs[:4], refs[4:8], refs[8:12]
    answers, scores = refs[12:16], refs[16]

    def body(place):
        far = []
        for ref in asked:
            both = ref[...].astype(F32)
            far += [both[:4], both[16:20]]
        mixed, peak, total = softmax_parts(
            jnp.concatenate(far, 0).astype(BF16),
            None,
            in_order(place, kv_refs),
            in_order(place, held_fresh(pack_refs, kv_refs[0].shape[0])),
            scores,
        )
        packed = pack_parts(mixed, peak, total)
        for i, ref in enumerate(answers):
            ref[...] = packed[8 * i : 8 * i + 8]

    each_place(me_ref, body)


SMEM = pl.BlockSpec(memory_space=pltpu.SMEM)


def attend_main(me, query, bounds, w_out, kv, packs):
    return pl.pallas_call(
        main_kernel,
        cost_estimate=COST,
        compiler_params=LIMIT,
        out_shape=(
            jax.ShapeDtypeStruct(query.shape, BF16),
            jax.ShapeDtypeStruct((8, 2 * HD), F32),
        ),
        in_specs=[SMEM] + [VMEM] * 11,
        out_specs=(VMEM,) * 2,
        scratch_shapes=[pltpu.VMEM((bounds.shape[0], kv[0].shape[1]), F32)],
    )(me, query, bounds, w_out, *kv, *packs)


def attend_far(me, kv, packs, asked):
    return pl.pallas_call(
        far_kernel,
        cost_estimate=COST,
        compiler_params=LIMIT,
        out_shape=(jax.ShapeDtypeStruct((8, 2 * HD), F32),) * 4,
        in_specs=[SMEM] + [VMEM] * 12,
        out_specs=(VMEM,) * 4,
        scratch_shapes=[pltpu.VMEM((32, kv[0].shape[1]), F32)],
    )(me, *kv, *packs, *asked)


def distance_of(flags_ref, distances):
    return jnp.where(flags_ref[2] == 0, distances[0], distances[1])


def pick_kernel(flags_ref, match_ref, *refs):
    far = jnp.zeros(refs[-1].shape, F32)
    group, groups = flags_ref[1], match_ref.shape[0]
    for ref, distances in zip(refs, DISTANCES):
        prompt = lax.rem(group + distance_of(flags_ref, distances) + groups, groups)
        far = jnp.where(match_ref[prompt] == group, ref[...], far)
    refs[-1][...] = far


def pick(flags, match, answers):
    return pl.pallas_call(
        pick_kernel,
        cost_estimate=COST,
        compiler_params=LIMIT,
        out_shape=jax.ShapeDtypeStruct(answers[0].shape, F32),
        in_specs=[SMEM] * 2 + [VMEM] * len(answers),
        out_specs=VMEM,
    )(flags, match, *answers)


def merge_kernel(flags_ref, attended_ref, own_ref, far_ref, mate_ref, perm_ref, w_ref, keep_ref, give_ref):
    own = own_ref[...]
    far = far_ref[:4] + mate_ref[4:]
    far = jnp.concatenate([far, far], 0)
    split = lambda packed: (
        packed[:, :HD], packed[:, HD : HD + 1], packed[:, 2 * HD - 1 : 2 * HD]
    )
    mixed_a, peak_a, total_a = split(own)
    mixed_b, peak_b, total_b = split(far)
    peak = jnp.maximum(peak_a, peak_b)
    scale_a = jnp.exp(peak_a - peak)
    scale_b = jnp.exp(peak_b - peak)
    ready = (mixed_a * scale_a + mixed_b * scale_b) / (total_a * scale_a + total_b * scale_b)
    ready = jnp.concatenate([ready[:STEPS], ready[STEPS : 2 * STEPS]], 1)
    attended = attended_ref[...]
    rows = attended.shape[0]
    lead = jnp.concatenate([ready] + [jnp.zeros_like(ready)] * (rows // STEPS - 1), 0)
    row = lax.broadcasted_iota(jnp.int32, lead.shape, 0)
    swap = (row < STEPS) & (flags_ref[0] == 1)
    attended = jnp.where(swap, lead, attended.astype(F32)).astype(BF16)
    attended = lax.dot_general(
        perm_ref[...], attended, (((0,), (0,)), ((), ())), preferred_element_type=F32
    ).astype(BF16)
    keep_ref[...] = attended[: rows // 2]
    shares_kernel_body(attended[rows // 2 :], w_ref, give_ref)


def shares_kernel_body(attended, w_ref, out_ref):
    width = 1024
    for first in range(0, w_ref.shape[1], width):
        span = slice(first, first + width)
        out_ref[:, span] = jnp.dot(attended, w_ref[:, span], preferred_element_type=F32).astype(BF16)


def shares_kernel(attended_ref, w_ref, out_ref):
    shares_kernel_body(attended_ref[...], w_ref, out_ref)


def shares(attended, w_out):
    return pl.pallas_call(
        shares_kernel,
        cost_estimate=COST,
        compiler_params=LIMIT,
        out_shape=jax.ShapeDtypeStruct((attended.shape[0], w_out.shape[1]), BF16),
        in_specs=[VMEM] * 2,
        out_specs=VMEM,
    )(attended, w_out)


def merge(flags, attended, own, far, mate, perm, w_out):
    half = jax.ShapeDtypeStruct((attended.shape[0] // 2, w_out.shape[1]), BF16)
    return pl.pallas_call(
        merge_kernel,
        cost_estimate=COST,
        compiler_params=LIMIT,
        out_shape=(jax.ShapeDtypeStruct((half.shape[0], attended.shape[1]), BF16), half),
        in_specs=[SMEM] + [VMEM] * 6,
        out_specs=(VMEM,) * 2,
    )(flags, attended, own, far, mate, perm, w_out)


def add_core_kernel(own_ref, across_ref, *out_refs):
    total = own_ref[...].astype(F32) + across_ref[...].astype(F32)
    width = total.shape[0] // len(out_refs)
    for i, ref in enumerate(out_refs):
        ref[...] = total[i * width : (i + 1) * width].astype(BF16)


def add_core(own, across):
    rows, columns = own.shape
    return pl.pallas_call(
        add_core_kernel,
        cost_estimate=COST,
        compiler_params=LIMIT,
        out_shape=(jax.ShapeDtypeStruct((rows // XN, columns), BF16),) * XN,
        in_specs=[VMEM, VMEM],
        out_specs=(VMEM,) * XN,
    )(own, across)


def add_x_kernel(a_ref, b_ref, c_ref, d_ref, own_ref, send_ref):
    total = a_ref[...].astype(F32)
    for ref in (b_ref, c_ref, d_ref):
        total = total + ref[...].astype(F32)
    half = total.shape[0] // 2
    own_ref[...] = total[:half]
    send_ref[...] = total[half:].astype(BF16)


def add_x(parts):
    rows, columns = parts[0].shape
    return pl.pallas_call(
        add_x_kernel,
        cost_estimate=COST,
        compiler_params=LIMIT,
        out_shape=(
            jax.ShapeDtypeStruct((rows // 2, columns), F32),
            jax.ShapeDtypeStruct((rows // 2, columns), BF16),
        ),
        in_specs=[VMEM] * 4,
        out_specs=(VMEM,) * 2,
    )(*parts)


def pick_row(table, selector):
    return jnp.sum(jnp.where(selector, table[None, :], 0), 1)


def carry(distances, groups, count, back):
    route = []
    for group in range(groups):
        for tp in range(count):
            far = (group + distances[tp % 2]) % groups
            asking = (groups + group) * count + tp
            asked = far * count + tp
            route.append((asked, asking) if back else (asking, asked))
    return route


def local(hidden, norm_gain, w_query, w_keyval, w_out, kv_cache, match, cache_lengths):
    side = lax.axis_index("role")
    group = lax.axis_index("grp")
    tp = lax.axis_index("tp")
    groups = lax.axis_size("grp")
    count = lax.axis_size("tp")
    own_rows = hidden[0, 0]
    block = own_rows.shape[0]
    row_count = block * count
    kv_t = kv_cache[0, 0].T
    cache_len = kv_t.shape[1]
    qcols = w_query.shape[1]
    kcols = w_keyval.shape[1]

    beside = lax.ppermute(own_rows, "tp", YHI)
    staged = stage(stage_kernel, own_rows)
    gain = stage(keep_kernel, after(norm_gain[None, :], staged))
    beside = after(beside, staged, gain)
    kv_sent = after(kv_t, staged)
    kv_y = lax.ppermute(kv_sent, "tp", YHI)
    kv_core = lax.ppermute(kv_sent, "tp", CORE)
    pair = norm(staged, gain, beside)
    others = {k: lax.ppermute(pair, "tp", xshift(-k)) for k in X_ORDER}
    others = [others[k] for k in range(1, XN)]
    token = touch(pair, w_query, w_keyval.T)
    others = after(others, kv_y, token)
    own_half = jnp.concatenate([pair] + others, 0)
    mate_half = after(lax.ppermute(own_half, "tp", CORE), kv_core)
    kv_both = lax.ppermute(kv_y, "tp", CORE)

    slot = jnp.arange(row_count, dtype=jnp.int32)
    piece = slot // block
    far_core, far_x, far_y = piece // 8, piece // 2 % XN, piece % 2
    owner = (
        (tp // 4 + far_x) % XN * 4
        + jnp.bitwise_xor(tp // 2 % 2, far_y) * 2
        + jnp.bitwise_xor(tp % 2, far_core)
    )
    row_at = owner * block + slot % block
    row_ids = jnp.arange(row_count, dtype=jnp.int32)
    placed = row_at[None, :] == row_ids[:, None]
    perm = placed.astype(BF16)

    request = row_ids // STEPS
    step_ids = row_ids % STEPS
    lengths = after(cache_lengths[0], pair)
    zero_one = jnp.zeros((1,), jnp.int32)
    bases = jnp.concatenate([jnp.full((1,), cache_len + row_count, jnp.int32), lengths])
    before = jnp.arange(lengths.shape[0])[None, :] < jnp.arange(lengths.shape[0])[:, None]
    offsets = pick_row(lengths, before)
    selector = request[:, None] == jnp.arange(row_count // STEPS, dtype=jnp.int32)[None, :]
    start = pick_row(jnp.concatenate([zero_one, offsets]), selector)
    span = pick_row(jnp.concatenate([zero_one, lengths]), selector)
    positions = jnp.where(side == 0, cache_len + row_ids, pick_row(bases, selector) + step_ids)
    low = jnp.where(side == 0, 0, start)
    high = jnp.where(side == 0, cache_len, start + span)
    fresh_low = jnp.where(side == 0, 0, request * STEPS)
    bounds = jnp.stack([low, high, fresh_low, row_ids], 1)
    bounds = jnp.concatenate([bounds, bounds], 0)

    position_at = jnp.sum(jnp.where(placed, positions[:, None], 0), 0).astype(F32)
    column = jnp.arange(qcols, dtype=jnp.int32)
    inverse = 500000.0 ** (-(2.0 / HD) * (column % HD // 2).astype(F32))
    angles = position_at[:, None] * inverse[None, :]
    cq = jnp.cos(angles)
    sq = jnp.sin(angles) * jnp.where(column % 2 == 0, -1.0, 1.0)[None, :]
    column = tp * kcols + jnp.arange(kcols, dtype=jnp.int32)
    inverse = 500000.0 ** (-(2.0 / HD) * (column % HD // 2).astype(F32))
    angles = inverse[:, None] * position_at[None, :]
    is_key = (column // HD % 2 == 0)[:, None]
    ck = jnp.where(is_key, jnp.cos(angles), 1.0)
    sk = jnp.where(is_key, jnp.sin(angles) * jnp.where(column % 2 == 0, -1.0, 1.0)[:, None], 0.0)

    query, pack = project(own_half, mate_half, w_query, w_keyval.T, cq, sq, ck, sk, perm, token)

    y_pack = lax.ppermute(pack, "tp", YHI)
    mate_pack = lax.ppermute(pack, "tp", CORE)
    packs = [pack, mate_pack, y_pack, lax.ppermute(y_pack, "tp", CORE)]
    leads = after(jnp.concatenate([pack[kcols:], mate_pack[kcols:]], 0), kv_both)
    axes = ("role", "grp", "tp")
    asked = [lax.ppermute(leads, axes, carry(d, groups, count, False)) for d in DISTANCES]
    kv = [kv_t, kv_core, kv_y, kv_both]
    me = jnp.reshape(tp % 4, (1,)).astype(jnp.int32)
    flags = jnp.stack([side, group, tp % 2]).astype(jnp.int32)
    answers = attend_far(me, kv, packs, asked)
    answers = [
        lax.ppermute(answer, axes, carry(d, groups, count, True))
        for answer, d in zip(answers, DISTANCES)
    ]
    query = after(query, asked)
    attended, lead_own = attend_main(me, query, bounds, w_out, kv, packs)

    answers = after(answers, attended)
    far = pick(flags, match, answers)
    mate = lax.ppermute(far, "tp", CORE)
    keep, give = merge(flags, attended, lead_own, far, mate, perm, w_out)

    across = lax.ppermute(give, "tp", CORE)
    keep = shares(keep, w_out)
    parts = add_core(keep, across)
    sent = {k: lax.ppermute(parts[k], "tp", xshift(k)) for k in X_ORDER}
    parts = [parts[0]] + [sent[k] for k in X_ORDER]
    summed, send = add_x(parts)
    summed = summed + lax.ppermute(send, "tp", YHI).astype(F32)
    return (own_rows.astype(F32) + summed).astype(BF16)[None, None]


def solution(mesh):
    return jax.shard_map(
        local,
        mesh=mesh,
        in_specs=(
            P("role", "grp", "tp", None),
            P(),
            P(None, "tp"),
            P(None, "tp"),
            P("tp", None),
            P("role", "grp", None, "tp"),
            P(),
            P("grp", None),
        ),
        out_specs=P("role", "grp", "tp", None),
        check_vma=False,
    )
```

```python
import functools
import math

import jax
import jax.numpy as jnp
from jax import lax
from jax.experimental import pallas as pl
from jax.experimental.pallas import tpu as pltpu
from jax.sharding import PartitionSpec as P

HD = 128
STEPS = 2
XN = 4
X_ORDER = (2, 1, 3)
NEG = -math.inf
F32 = jnp.float32
BF16 = jnp.bfloat16
VMEM = pl.BlockSpec(memory_space=pltpu.VMEM)
LIMIT = pltpu.CompilerParams(vmem_limit_bytes=8 * 1024 * 1024)
COST = pl.CostEstimate(flops=1, bytes_accessed=1, transcendentals=0)

CORE = [(i, i ^ 1) for i in range(16)]
YHI = [(i, i ^ 2) for i in range(16)]
BOTH = [(i, i ^ 3) for i in range(16)]


def xshift(k):
    return [(i, (i + 4 * k) % 16) for i in range(16)]


DISTANCES = ((3, 4), (-2, -3), (1, 2), (0, -1))


def after(value, *others):
    return lax.optimization_barrier((value,) + others)[0]


def scaled(rows):
    floated = rows.astype(F32)
    spread = jnp.mean(floated * floated, axis=-1, keepdims=True)
    return floated * lax.rsqrt(spread + 1e-05)


def stage_kernel(own_ref, out_ref):
    out_ref[...] = scaled(own_ref[...])


def keep_kernel(gain_ref, kept_ref):
    kept_ref[...] = gain_ref[...]


def norm_kernel(own_ref, gain_ref, beside_ref, out_ref):
    both = jnp.concatenate([own_ref[...], scaled(beside_ref[...])], 0)
    out_ref[...] = (both * gain_ref[...]).astype(BF16)


def stage(kernel, value):
    return pl.pallas_call(
        kernel,
        cost_estimate=COST,
        compiler_params=LIMIT,
        out_shape=jax.ShapeDtypeStruct(value.shape, F32),
        in_specs=[VMEM],
        out_specs=VMEM,
    )(value)


def norm(own, gain, beside):
    return pl.pallas_call(
        norm_kernel,
        cost_estimate=COST,
        compiler_params=LIMIT,
        out_shape=jax.ShapeDtypeStruct((2 * own.shape[0], own.shape[1]), BF16),
        in_specs=[VMEM] * 3,
        out_specs=VMEM,
    )(own, gain, beside)


def touch_kernel(*refs):
    refs[-1][...] = jnp.zeros(refs[-1].shape, F32)


def touch(*arrays):
    return pl.pallas_call(
        touch_kernel,
        cost_estimate=COST,
        compiler_params=LIMIT,
        out_shape=jax.ShapeDtypeStruct((8, HD), F32),
        in_specs=[VMEM] * len(arrays),
        out_specs=VMEM,
    )(*arrays)


def turn(value, cosine, sine, axis):
    size = value.shape[axis]
    index = lax.broadcasted_iota(jnp.int32, value.shape, axis)
    ahead = pltpu.roll(value, size - 1, axis)
    behind = pltpu.roll(value, 1, axis)
    return value * cosine + jnp.where(index % 2 == 0, ahead, behind) * sine


def project_kernel(
    own_ref, mate_ref, wq_ref, wkv_ref, cq_ref, sq_ref, ck_ref, sk_ref, perm_ref,
    token_ref, q_ref, pack_ref,
):
    del token_ref
    rows = jnp.concatenate([own_ref[...], mate_ref[...]], 0)
    query = jnp.dot(rows, wq_ref[...], preferred_element_type=F32)
    fresh = lax.dot_general(
        wkv_ref[...], rows, (((1,), (1,)), ((), ())), preferred_element_type=F32
    )
    perm = perm_ref[...]
    query = turn(query, cq_ref[...], sq_ref[...], 1).astype(BF16)
    query = jnp.dot(perm, query, preferred_element_type=F32)
    q_ref[...] = query.astype(BF16)
    fresh = turn(fresh, ck_ref[...], sk_ref[...], 0).astype(BF16)
    fresh = lax.dot_general(fresh, perm, (((1,), (1,)), ((), ())), preferred_element_type=F32)
    size = fresh.shape[0]
    pack_ref[:size, :] = jnp.concatenate([fresh, jnp.zeros_like(fresh)], 1).astype(BF16)
    lead = lead_rows(query[:, :HD], query[:, HD:])
    pack_ref[size:, :] = jnp.concatenate([lead, jnp.zeros_like(lead)], 0).astype(BF16)


def lead_rows(first, second):
    both = jnp.concatenate([first[:STEPS], second[:STEPS]], 0)
    return jnp.concatenate([both, jnp.zeros_like(both)], 0)


def project(own, mate, w_query, w_kv_t, cq, sq, ck, sk, perm, token):
    rows = 2 * own.shape[0]
    return pl.pallas_call(
        project_kernel,
        cost_estimate=COST,
        compiler_params=LIMIT,
        out_shape=(
            jax.ShapeDtypeStruct((rows, w_query.shape[1]), BF16),
            jax.ShapeDtypeStruct((w_kv_t.shape[0] + 16, HD), BF16),
        ),
        in_specs=[VMEM] * 10,
        out_specs=(VMEM,) * 2,
    )(own, mate, w_query, w_kv_t, cq, sq, ck, sk, perm, token)


def softmax_parts(queries, bounds, kv_refs, fresh, scores):
    tokens = kv_refs[0].shape[1]
    chunk = 512
    scale = 1.0 / math.sqrt(HD)
    if bounds is not None:
        low, high, fresh_low, fresh_high = bounds

    def pair(first, span):
        return jnp.concatenate([kv_refs[first][:, span], kv_refs[first + 1][:, span]], 0)

    fresh_keys = jnp.concatenate(fresh[:2], 0)
    fresh_values = jnp.concatenate(fresh[2:], 0)
    fresh_scores = jnp.dot(queries, fresh_keys, preferred_element_type=F32) * scale
    if bounds is not None:
        index = lax.broadcasted_iota(jnp.int32, fresh_scores.shape, 1)
        fresh_scores = jnp.where((index >= fresh_low) & (index <= fresh_high), fresh_scores, NEG)
    peak = jnp.max(fresh_scores, -1, keepdims=True)
    for start in range(0, tokens, chunk):
        span = slice(start, start + chunk)
        part_scores = jnp.dot(queries, pair(0, span), preferred_element_type=F32) * scale
        if bounds is not None:
            index = lax.broadcasted_iota(jnp.int32, part_scores.shape, 1) + start
            part_scores = jnp.where((index >= low) & (index < high), part_scores, NEG)
        scores[:, span] = part_scores
        peak = jnp.maximum(peak, jnp.max(part_scores, -1, keepdims=True))
    contract = (((1,), (1,)), ((), ()))
    weights = jnp.exp(fresh_scores - peak)
    total = jnp.sum(weights, -1, keepdims=True)
    mixed = lax.dot_general(
        weights.astype(BF16), fresh_values, contract, preferred_element_type=F32
    )
    for start in range(0, tokens, chunk):
        span = slice(start, start + chunk)
        weights = jnp.exp(scores[:, span] - peak)
        total += jnp.sum(weights, -1, keepdims=True)
        mixed += lax.dot_general(
            weights.astype(BF16), pair(2, span), contract, preferred_element_type=F32
        )
    return mixed, peak, total


def pack_parts(mixed, peak, total):
    lane = lax.broadcasted_iota(jnp.int32, mixed.shape, 1)
    return jnp.concatenate([mixed, jnp.where(lane < HD // 2, peak, total)], 1)


def in_order(place, held):
    return [held[place ^ part] for part in range(4)]


def each_place(body):
    here = lax.rem(lax.axis_index("tp"), 4)
    for place in range(4):
        pl.when(here == place)(functools.partial(body, place))


def held_fresh(pack_refs, size):
    return [ref[:size, :size] for ref in pack_refs]


def main_kernel(q_ref, bounds_ref, w_ref, *refs):
    del w_ref
    kv_refs, pack_refs = refs[:4], refs[4:8]
    out_ref, lead_ref, scores = refs[8:]

    def body(place):
        query = q_ref[...]
        rows = query.shape[0]
        bounds = bounds_ref[...]
        mixed, peak, total = softmax_parts(
            jnp.concatenate([query[:, :HD], query[:, HD:]], 0),
            [bounds[:, i : i + 1] for i in range(4)],
            in_order(place, kv_refs),
            in_order(place, held_fresh(pack_refs, kv_refs[0].shape[0])),
            scores,
        )
        ready = mixed / total
        out_ref[...] = jnp.concatenate([ready[:rows], ready[rows:]], 1).astype(BF16)
        packed = pack_parts(mixed, peak, total)
        lead_ref[...] = lead_rows(packed[:8], packed[rows : rows + 8])

    each_place(body)


def far_kernel(*refs):
    kv_refs, pack_refs, asked = refs[:4], refs[4:8], refs[8:12]
    answers, scores = refs[12:16], refs[16]

    def body(place):
        far = []
        for ref in asked:
            both = ref[...].astype(F32)
            far += [both[:4], both[16:20]]
        mixed, peak, total = softmax_parts(
            jnp.concatenate(far, 0).astype(BF16),
            None,
            in_order(place, kv_refs),
            in_order(place, held_fresh(pack_refs, kv_refs[0].shape[0])),
            scores,
        )
        packed = pack_parts(mixed, peak, total)
        for i, ref in enumerate(answers):
            ref[...] = packed[8 * i : 8 * i + 8]

    each_place(body)


SMEM = pl.BlockSpec(memory_space=pltpu.SMEM)


def attend_main(query, bounds, w_out, kv, packs):
    return pl.pallas_call(
        main_kernel,
        cost_estimate=COST,
        compiler_params=LIMIT,
        out_shape=(
            jax.ShapeDtypeStruct(query.shape, BF16),
            jax.ShapeDtypeStruct((8, 2 * HD), F32),
        ),
        in_specs=[VMEM] * 11,
        out_specs=(VMEM,) * 2,
        scratch_shapes=[pltpu.VMEM((bounds.shape[0], kv[0].shape[1]), F32)],
    )(query, bounds, w_out, *kv, *packs)


def attend_far(kv, packs, asked):
    return pl.pallas_call(
        far_kernel,
        cost_estimate=COST,
        compiler_params=LIMIT,
        out_shape=(jax.ShapeDtypeStruct((8, 2 * HD), F32),) * 4,
        in_specs=[VMEM] * 12,
        out_specs=(VMEM,) * 4,
        scratch_shapes=[pltpu.VMEM((32, kv[0].shape[1]), F32)],
    )(*kv, *packs, *asked)


def distance_of(distances):
    return jnp.where(lax.rem(lax.axis_index("tp"), 2) == 0, distances[0], distances[1])


def pick_kernel(match_ref, *refs):
    far = jnp.zeros(refs[-1].shape, F32)
    group, groups = lax.axis_index("grp"), match_ref.shape[0]
    for ref, distances in zip(refs, DISTANCES):
        prompt = lax.rem(group + distance_of(distances) + groups, groups)
        far = jnp.where(match_ref[prompt] == group, ref[...], far)
    refs[-1][...] = far


def pick(match, answers):
    return pl.pallas_call(
        pick_kernel,
        cost_estimate=COST,
        compiler_params=LIMIT,
        out_shape=jax.ShapeDtypeStruct(answers[0].shape, F32),
        in_specs=[SMEM] + [VMEM] * len(answers),
        out_specs=VMEM,
    )(match, *answers)


def merge_kernel(attended_ref, own_ref, far_ref, mate_ref, perm_ref, w_ref, keep_ref, give_ref):
    own = own_ref[...]
    far = far_ref[:4] + mate_ref[4:]
    far = jnp.concatenate([far, far], 0)
    split = lambda packed: (
        packed[:, :HD], packed[:, HD : HD + 1], packed[:, 2 * HD - 1 : 2 * HD]
    )
    mixed_a, peak_a, total_a = split(own)
    mixed_b, peak_b, total_b = split(far)
    peak = jnp.maximum(peak_a, peak_b)
    scale_a = jnp.exp(peak_a - peak)
    scale_b = jnp.exp(peak_b - peak)
    ready = (mixed_a * scale_a + mixed_b * scale_b) / (total_a * scale_a + total_b * scale_b)
    ready = jnp.concatenate([ready[:STEPS], ready[STEPS : 2 * STEPS]], 1)
    attended = attended_ref[...]
    rows = attended.shape[0]
    lead = jnp.concatenate([ready] + [jnp.zeros_like(ready)] * (rows // STEPS - 1), 0)
    row = lax.broadcasted_iota(jnp.int32, lead.shape, 0)
    swap = (row < STEPS) & (lax.axis_index("role") == 1)
    attended = jnp.where(swap, lead, attended.astype(F32)).astype(BF16)
    attended = lax.dot_general(
        perm_ref[...], attended, (((0,), (0,)), ((), ())), preferred_element_type=F32
    ).astype(BF16)
    keep_ref[...] = attended[: rows // 2]
    shares_kernel_body(attended[rows // 2 :], w_ref, give_ref)


def shares_kernel_body(attended, w_ref, out_ref):
    width = 1024
    for first in range(0, w_ref.shape[1], width):
        span = slice(first, first + width)
        out_ref[:, span] = jnp.dot(attended, w_ref[:, span], preferred_element_type=F32).astype(BF16)


def shares_kernel(attended_ref, w_ref, out_ref):
    shares_kernel_body(attended_ref[...], w_ref, out_ref)


def shares(attended, w_out):
    return pl.pallas_call(
        shares_kernel,
        cost_estimate=COST,
        compiler_params=LIMIT,
        out_shape=jax.ShapeDtypeStruct((attended.shape[0], w_out.shape[1]), BF16),
        in_specs=[VMEM] * 2,
        out_specs=VMEM,
    )(attended, w_out)


def merge(attended, own, far, mate, perm, w_out):
    half = jax.ShapeDtypeStruct((attended.shape[0] // 2, w_out.shape[1]), BF16)
    return pl.pallas_call(
        merge_kernel,
        cost_estimate=COST,
        compiler_params=LIMIT,
        out_shape=(jax.ShapeDtypeStruct((half.shape[0], attended.shape[1]), BF16), half),
        in_specs=[VMEM] * 6,
        out_specs=(VMEM,) * 2,
    )(attended, own, far, mate, perm, w_out)


def add_core_kernel(own_ref, across_ref, *out_refs):
    total = own_ref[...].astype(F32) + across_ref[...].astype(F32)
    width = total.shape[0] // len(out_refs)
    for i, ref in enumerate(out_refs):
        ref[...] = total[i * width : (i + 1) * width].astype(BF16)


def add_core(own, across):
    rows, columns = own.shape
    return pl.pallas_call(
        add_core_kernel,
        cost_estimate=COST,
        compiler_params=LIMIT,
        out_shape=(jax.ShapeDtypeStruct((rows // XN, columns), BF16),) * XN,
        in_specs=[VMEM, VMEM],
        out_specs=(VMEM,) * XN,
    )(own, across)


def add_x_kernel(a_ref, b_ref, c_ref, d_ref, own_ref, send_ref):
    total = a_ref[...].astype(F32)
    for ref in (b_ref, c_ref, d_ref):
        total = total + ref[...].astype(F32)
    half = total.shape[0] // 2
    own_ref[...] = total[:half]
    send_ref[...] = total[half:].astype(BF16)


def add_x(parts):
    rows, columns = parts[0].shape
    return pl.pallas_call(
        add_x_kernel,
        cost_estimate=COST,
        compiler_params=LIMIT,
        out_shape=(
            jax.ShapeDtypeStruct((rows // 2, columns), F32),
            jax.ShapeDtypeStruct((rows // 2, columns), BF16),
        ),
        in_specs=[VMEM] * 4,
        out_specs=(VMEM,) * 2,
    )(*parts)


def pick_row(table, selector):
    return jnp.sum(jnp.where(selector, table[None, :], 0), 1)


def carry(distances, groups, count, back):
    route = []
    for group in range(groups):
        for tp in range(count):
            far = (group + distances[tp % 2]) % groups
            asking = (groups + group) * count + tp
            asked = far * count + tp
            route.append((asked, asking) if back else (asking, asked))
    return route


def local(hidden, norm_gain, w_query, w_keyval, w_out, kv_cache, match, cache_lengths):
    side = lax.axis_index("role")
    group = lax.axis_index("grp")
    tp = lax.axis_index("tp")
    groups = lax.axis_size("grp")
    count = lax.axis_size("tp")
    own_rows = hidden[0, 0]
    block = own_rows.shape[0]
    row_count = block * count
    kv_t = kv_cache[0, 0].T
    cache_len = kv_t.shape[1]
    qcols = w_query.shape[1]
    kcols = w_keyval.shape[1]

    beside = lax.ppermute(own_rows, "tp", YHI)
    staged = stage(stage_kernel, own_rows)
    gain = stage(keep_kernel, after(norm_gain[None, :], staged))
    beside = after(beside, staged, gain)
    kv_sent = after(kv_t, staged)
    kv_y = lax.ppermute(kv_sent, "tp", YHI)
    kv_core = lax.ppermute(kv_sent, "tp", CORE)
    pair = norm(staged, gain, beside)
    others = {k: lax.ppermute(pair, "tp", xshift(-k)) for k in X_ORDER}
    others = [others[k] for k in range(1, XN)]
    token = touch(pair, w_query, w_keyval.T)
    others = after(others, kv_y, token)
    own_half = jnp.concatenate([pair] + others, 0)
    mate_half = after(lax.ppermute(own_half, "tp", CORE), kv_core)
    kv_both = lax.ppermute(kv_y, "tp", CORE)

    slot = jnp.arange(row_count, dtype=jnp.int32)
    piece = slot // block
    far_core, far_x, far_y = piece // 8, piece // 2 % XN, piece % 2
    owner = (
        (tp // 4 + far_x) % XN * 4
        + jnp.bitwise_xor(tp // 2 % 2, far_y) * 2
        + jnp.bitwise_xor(tp % 2, far_core)
    )
    row_at = owner * block + slot % block
    row_ids = jnp.arange(row_count, dtype=jnp.int32)
    placed = row_at[None, :] == row_ids[:, None]
    perm = placed.astype(BF16)

    request = row_ids // STEPS
    step_ids = row_ids % STEPS
    lengths = after(cache_lengths[0], pair)
    zero_one = jnp.zeros((1,), jnp.int32)
    bases = jnp.concatenate([jnp.full((1,), cache_len + row_count, jnp.int32), lengths])
    before = jnp.arange(lengths.shape[0])[None, :] < jnp.arange(lengths.shape[0])[:, None]
    offsets = pick_row(lengths, before)
    selector = request[:, None] == jnp.arange(row_count // STEPS, dtype=jnp.int32)[None, :]
    start = pick_row(jnp.concatenate([zero_one, offsets]), selector)
    span = pick_row(jnp.concatenate([zero_one, lengths]), selector)
    positions = jnp.where(side == 0, cache_len + row_ids, pick_row(bases, selector) + step_ids)
    low = jnp.where(side == 0, 0, start)
    high = jnp.where(side == 0, cache_len, start + span)
    fresh_low = jnp.where(side == 0, 0, request * STEPS)
    bounds = jnp.stack([low, high, fresh_low, row_ids], 1)
    bounds = jnp.concatenate([bounds, bounds], 0)

    position_at = jnp.sum(jnp.where(placed, positions[:, None], 0), 0).astype(F32)
    column = jnp.arange(qcols, dtype=jnp.int32)
    inverse = 500000.0 ** (-(2.0 / HD) * (column % HD // 2).astype(F32))
    angles = position_at[:, None] * inverse[None, :]
    cq = jnp.cos(angles)
    sq = jnp.sin(angles) * jnp.where(column % 2 == 0, -1.0, 1.0)[None, :]
    column = tp * kcols + jnp.arange(kcols, dtype=jnp.int32)
    inverse = 500000.0 ** (-(2.0 / HD) * (column % HD // 2).astype(F32))
    angles = inverse[:, None] * position_at[None, :]
    is_key = (column // HD % 2 == 0)[:, None]
    ck = jnp.where(is_key, jnp.cos(angles), 1.0)
    sk = jnp.where(is_key, jnp.sin(angles) * jnp.where(column % 2 == 0, -1.0, 1.0)[:, None], 0.0)

    query, pack = project(own_half, mate_half, w_query, w_keyval.T, cq, sq, ck, sk, perm, token)

    y_pack = lax.ppermute(pack, "tp", YHI)
    mate_pack = lax.ppermute(pack, "tp", CORE)
    packs = [pack, mate_pack, y_pack, lax.ppermute(y_pack, "tp", CORE)]
    leads = after(jnp.concatenate([pack[kcols:], mate_pack[kcols:]], 0), kv_both)
    axes = ("role", "grp", "tp")
    asked = [lax.ppermute(leads, axes, carry(d, groups, count, False)) for d in DISTANCES]
    kv = [kv_t, kv_core, kv_y, kv_both]
    answers = attend_far(kv, packs, asked)
    answers = [
        lax.ppermute(answer, axes, carry(d, groups, count, True))
        for answer, d in zip(answers, DISTANCES)
    ]
    query = after(query, asked)
    attended, lead_own = attend_main(query, bounds, w_out, kv, packs)

    answers = after(answers, attended)
    far = pick(match, answers)
    mate = lax.ppermute(far, "tp", CORE)
    keep, give = merge(attended, lead_own, far, mate, perm, w_out)

    across = lax.ppermute(give, "tp", CORE)
    keep = shares(keep, w_out)
    parts = add_core(keep, across)
    sent = {k: lax.ppermute(parts[k], "tp", xshift(k)) for k in X_ORDER}
    parts = [parts[0]] + [sent[k] for k in X_ORDER]
    summed, send = add_x(parts)
    summed = summed + lax.ppermute(send, "tp", YHI).astype(F32)
    return (own_rows.astype(F32) + summed).astype(BF16)[None, None]


def solution(mesh):
    return jax.shard_map(
        local,
        mesh=mesh,
        in_specs=(
            P("role", "grp", "tp", None),
            P(),
            P(None, "tp"),
            P(None, "tp"),
            P("tp", None),
            P("role", "grp", None, "tp"),
            P(),
            P("grp", None),
        ),
        out_specs=P("role", "grp", "tp", None),
        check_vma=False,
    )
```
